32 devices in a mesh: freq: 8 (over y, x, core), stn: 4 (over z).
Axes of the slice: x: 2, y: 2, z: 4, core: 2. Of those that a mesh axis runs over, the one named last changes fastest.
Arguments:
- visibilities: float32 [8, 8, 256, 256], P('freq', None, 'stn'), may hold values from -6 to 6
- flag_mask: int32 [256, 256], P('stn'), may hold values 0 or 1
- stations: float32 [3, 256], P(None, 'stn'), may hold values from -32 to 32
- directions: float32 [2, 1536], replicated, may hold values from -0.5 to 0.5
- intensity: float32 [1536], replicated, may hold values from 0.02 to 0.2
- polarized: float32 [2, 1536], replicated, may hold values from -0.4375 to 0.4375
- spectral: float32 [1536], replicated, may hold values from -1.5 to 0.5
- clusters: int32 [1536], replicated, may hold values from 0 to 15, as said below
- jones_gains: float32 [8, 8, 16, 256], P('freq', None, None, 'stn'), may hold values from -6 to 6
- scaled_duals: float32 [8, 8, 16, 256], P('freq', None, None, 'stn'), may hold values from -4 to 4
- consensus: float32 [4, 8, 16, 256], P(None, None, None, 'stn'), may hold values from -6 to 6
Outputs:
- jones_next: float32 [8, 8, 16, 256], P('freq', None, None, 'stn')
- duals_next: float32 [8, 8, 16, 256], P('freq', None, None, 'stn')
- consensus_next: float32 [4, 8, 16, 256], P(None, None, None, 'stn')
The draws below stay inside these ranges and needn't reach their ends.
Inputs may be any that keep to these rules, and one draw needn't show every extreme that they name: `clusters`: every direction holds exactly 96 components.
All inputs are finite; a program needn't handle non-finite values. No bound on the sum of `flag_mask` on one device may be relied on, other than what follows from the above.
Results may differ from the reference program's by a relative error of at most 0.0019.
Values may be sent and summed in bfloat16 or wider, within the bound.
A program may use at most 64 MiB of HBM per device.

```python
import math
import jax
import jax.numpy as jnp
from jax import lax

DIRS = 16
COMPS = 1536
POLY = 4
NS = 256
FREQS = 8


def draw_clusters(key, part):
    key = jax.random.fold_in(key, 7)
    return (jax.random.permutation(key, COMPS) % DIRS).astype(jnp.int32)


def plant(values, own_key, low, largest):
    longest = values.shape.index(max(values.shape))
    spots = []
    for shift in (0, 1):
        where = [jax.random.randint(jax.random.fold_in(own_key, axis), (), 0, length) for axis, length in enumerate(values.shape)]
        where[longest] = (where[longest] + shift) % values.shape[longest]
        spots.append(tuple(where))
    return values.at[spots[0]].set(low).at[spots[1]].set(largest)


def steps_of(own_key, dims, shards, least, largest):
    level = 1.0
    for dim, blocks in shards:
        steps = jax.random.uniform(jax.random.fold_in(jax.random.fold_in(own_key, 6), dim), (blocks,), jnp.float32, least / len(shards), largest / len(shards))
        level = level * jnp.repeat(jnp.exp(steps), dims[dim] // blocks).reshape((-1,) + (1,) * (len(dims) - 1 - dim))
    return level


def gaussian(rng, extent, scale, bound, shards=(), held_as=jnp.bfloat16):
    values = jax.random.normal(rng, extent, jnp.float32) * scale
    if len(shards) > 0:
        values = steps_of(rng, extent, shards, -0.22, 0.18) * values
    return jnp.clip(values, min=-bound, max=bound).astype(held_as)


def setup_inputs(seed: int = 0) -> dict:
    key_of = jax.random.split(jax.random.key(seed), 12)
    return {
        "visibilities": gaussian(key_of[0], (FREQS, 8, NS, NS), 1.0, 6.0, ((0, 8), (2, 4)), jnp.float32),
        "flag_mask": plant((jax.random.randint(key_of[1], (NS, NS), 0, 8) < 7).astype(jnp.int32), jax.random.fold_in(key_of[1], 1), 0, 1),
        "stations": gaussian(key_of[2], (3, NS), 5.0, 32.0, ((1, 4),), jnp.float32),
        "directions": jnp.clip(jax.random.uniform(key_of[3], (2, COMPS), jnp.float32, -0.5, 0.5), -0.5, 0.5),
        "intensity": jnp.clip(jnp.exp(jax.random.uniform(key_of[4], (COMPS,), jnp.float32, math.log(0.02), math.log(0.2))), 0.02, 0.2),
        "polarized": gaussian(key_of[5], (2, COMPS), 0.03, 0.4375, (), jnp.float32),
        "spectral": jnp.clip(jax.random.uniform(key_of[6], (COMPS,), jnp.float32, -1.5, 0.5), -1.5, 0.5),
        "clusters": draw_clusters(jax.random.fold_in(key_of[11], 71), 0),
        "jones_gains": gaussian(key_of[8], (FREQS, 8, DIRS, NS), 0.7, 6.0, ((0, 8), (3, 4)), jnp.float32),
        "scaled_duals": gaussian(key_of[9], (FREQS, 8, DIRS, NS), 0.3, 4.0, ((0, 8), (3, 4)), jnp.float32),
        "consensus": gaussian(key_of[10], (POLY, 8, DIRS, NS), 0.4, 6.0, ((3, 4),), jnp.float32),
    }


TWO_PI = 6.283185307179586
PENALTY = 40.0
STEP_SIZE = 0.5

def complex_mul(lhs_value, rhs_value):
    return (lhs_value[0] * rhs_value[0] - lhs_value[1] * rhs_value[1], lhs_value[0] * rhs_value[1] + lhs_value[1] * rhs_value[0])

def complex_add(lhs_value, rhs_value):
    return (lhs_value[0] + rhs_value[0], lhs_value[1] + rhs_value[1])

def complex_conj(number):
    return (number[0], -number[1])

def matrix_mul(lhs_matrix, rhs_matrix):
    return [complex_add(complex_mul(lhs_matrix[0], rhs_matrix[0]), complex_mul(lhs_matrix[1], rhs_matrix[2])), complex_add(complex_mul(lhs_matrix[0], rhs_matrix[1]), complex_mul(lhs_matrix[1], rhs_matrix[3])), complex_add(complex_mul(lhs_matrix[2], rhs_matrix[0]), complex_mul(lhs_matrix[3], rhs_matrix[2])), complex_add(complex_mul(lhs_matrix[2], rhs_matrix[1]), complex_mul(lhs_matrix[3], rhs_matrix[3]))]

def matrix_herm(matrix):
    return [complex_conj(matrix[0]), complex_conj(matrix[2]), complex_conj(matrix[1]), complex_conj(matrix[3])]

def unpack_matrix(stacked):
    return [(stacked[0], stacked[1]), (stacked[2], stacked[3]), (stacked[4], stacked[5]), (stacked[6], stacked[7])]

def pack_matrix(matrix):
    return jnp.stack([member for element in matrix for member in element])

def summed_pack(matrix, reduce_dim):
    return -jnp.stack([lax.optimization_barrier(jnp.sum(member, reduce_dim)) for element in matrix for member in element])

def band_ratio(index_value, band_count):
    return 0.5 + 3.0 * (index_value.astype(jnp.float32) + 0.5) / band_count

def phase_table(positions, sky_dirs, freq_ratio):
    dir_l = sky_dirs[0][:, None]
    dir_m = sky_dirs[1][:, None]
    dir_n = jnp.sqrt(1.0 - dir_l * dir_l - dir_m * dir_m)
    geometry = dir_l * positions[0][None, :] + dir_m * positions[1][None, :] + (dir_n - 1.0) * positions[2][None, :]
    phase_angle = TWO_PI * freq_ratio * geometry
    return jnp.stack([jnp.cos(phase_angle), -jnp.sin(phase_angle)]).astype(jnp.bfloat16)

def flux_weights(intensity, polarized, spectral, freq_ratio):
    factor = jnp.power(freq_ratio, spectral)
    return jnp.stack([(intensity + polarized[0]) * factor, polarized[1] * factor, (intensity - polarized[0]) * factor])

def legendre_table(band_count):
    centre = (2.0 * jnp.arange(band_count, dtype=jnp.float32) + 1.0) / band_count - 1.0
    return jnp.stack([jnp.ones_like(centre), centre, 0.5 * (3.0 * centre * centre - 1.0), 0.5 * (5.0 * centre * centre * centre - 3.0 * centre)], axis=1)

def gram_solve(gram_matrix, rhs_rows):
    chol_lower = jnp.linalg.cholesky(gram_matrix)
    forward = []
    for row_at in range(4):
        current = rhs_rows[row_at]
        for col_at in range(row_at):
            current = current - chol_lower[row_at, col_at] * forward[col_at]
        forward.append(current / chol_lower[row_at, row_at])
    backward = [forward[0]] * 4
    for row_at in (3, 2, 1, 0):
        current = forward[row_at]
        for col_at in range(row_at + 1, 4):
            current = current - chol_lower[col_at, row_at] * backward[col_at]
        backward[row_at] = current / chol_lower[row_at, row_at]
    return jnp.stack(backward)

def coherence(direction, own_table, all_table, weights, block_span):
    offset = direction * block_span
    own_real = lax.dynamic_slice_in_dim(own_table[0], offset, block_span, 0)
    own_imag = lax.dynamic_slice_in_dim(own_table[1], offset, block_span, 0)
    weight_block = lax.dynamic_slice_in_dim(weights, offset, block_span, 1)
    blocks = []
    for flux_at in range(3):
        factor_col = weight_block[flux_at][:, None]
        blocks.append(jnp.concatenate([own_real * factor_col, own_imag * factor_col], 0).astype(jnp.bfloat16))
    operand_left = jnp.concatenate(blocks, 1)
    far_real = lax.dynamic_slice_in_dim(all_table[0], offset, block_span, 0)
    far_imag = lax.dynamic_slice_in_dim(all_table[1], offset, block_span, 0)
    operand_right = jnp.concatenate([jnp.concatenate([far_real, -far_imag], 1), jnp.concatenate([far_imag, far_real], 1)], 0)
    product = lax.dot_general(operand_left.astype(jnp.float32), operand_right.astype(jnp.float32), (((0,), (0,)), ((), ())), precision=lax.Precision.HIGHEST, preferred_element_type=jnp.float32)
    row_count = own_real.shape[1]
    col_count = far_real.shape[1]
    entries = [(product[flux_at * row_count:(flux_at + 1) * row_count, :col_count], product[flux_at * row_count:(flux_at + 1) * row_count, col_count:]) for flux_at in range(3)]
    return [entries[0], entries[1], entries[1], entries[2]]

def residual_of(band_vis, mask_float, near_gains, far_gains, own_table, all_table, weights, block_span):

    def direction_step(model_sum, direction):
        coh_matrix = coherence(direction, own_table, all_table, weights, block_span)
        near_jones = unpack_matrix(lax.dynamic_index_in_dim(near_gains, direction, 1, keepdims=False)[:, :, None])
        far_jones = unpack_matrix(lax.dynamic_index_in_dim(far_gains, direction, 1, keepdims=False)[:, None, :])
        model_term = matrix_mul(matrix_mul(near_jones, coh_matrix), matrix_herm(far_jones))
        return (model_sum + pack_matrix(model_term), None)
    model_sum, _ = lax.scan(direction_step, jnp.zeros(band_vis.shape, jnp.float32), jnp.arange(near_gains.shape[1], dtype=jnp.int32))
    return (band_vis - model_sum) * mask_float[None]

def gradient_of(residual, near_gains, far_gains, own_table, all_table, weights, block_span):
    res_matrix = unpack_matrix(residual)

    def direction_step(state_value, direction):
        coh_matrix = coherence(direction, own_table, all_table, weights, block_span)
        near_jones = unpack_matrix(lax.dynamic_index_in_dim(near_gains, direction, 1, keepdims=False)[:, :, None])
        far_jones = unpack_matrix(lax.dynamic_index_in_dim(far_gains, direction, 1, keepdims=False)[:, None, :])
        col_part = matrix_mul(matrix_herm(res_matrix), matrix_mul(near_jones, coh_matrix))
        row_part = matrix_mul(res_matrix, matrix_mul(far_jones, matrix_herm(coh_matrix)))
        return (state_value, (summed_pack(row_part, 1), summed_pack(col_part, 0)))
    _, (row_terms, col_terms) = lax.scan(direction_step, jnp.zeros((), jnp.float32), jnp.arange(near_gains.shape[1], dtype=jnp.int32))
    return (row_terms, col_terms)

def reference(visibilities, flag_mask, stations, directions, intensity, polarized, spectral, clusters, jones_gains, scaled_duals, consensus):
    sort_order = jnp.argsort(clusters, stable=True)
    sky_dirs = directions[:, sort_order]
    sky_flux = intensity[sort_order]
    sky_pol = polarized[:, sort_order]
    sky_index = spectral[sort_order]
    block_span = COMPS // DIRS
    mask_float = flag_mask.astype(jnp.float32)
    basis_table = legendre_table(FREQS)

    def one_band(band_item):
        band_index, band_vis, band_jones, band_duals, basis_row = band_item
        freq_ratio = band_ratio(band_index, FREQS)
        phase_tab = phase_table(stations, sky_dirs, freq_ratio)
        weights = flux_weights(sky_flux, sky_pol, sky_index, freq_ratio)
        residual = residual_of(band_vis, mask_float, band_jones, band_jones, phase_tab, phase_tab, weights, block_span)
        row_terms, col_terms = gradient_of(residual, band_jones, band_jones, phase_tab, phase_tab, weights, block_span)
        poly_value = lax.optimization_barrier(jnp.sum(basis_row[:, None, None, None] * consensus, 0))
        drive = jnp.transpose(row_terms + col_terms, (1, 0, 2)) + PENALTY / 2.0 * (band_jones - poly_value + band_duals)
        step_length = STEP_SIZE / jnp.sqrt(jnp.sum(drive * drive) / drive.size + 1e-06)
        return band_jones - step_length * drive
    jones_next = lax.map(one_band, (jnp.arange(FREQS, dtype=jnp.int32), visibilities, jones_gains, scaled_duals, basis_table))
    summed = jnp.einsum('fi,fckn->ickn', basis_table, jones_next + scaled_duals, precision=lax.Precision.HIGHEST)
    gram_matrix = jnp.dot(basis_table.T, basis_table, precision=lax.Precision.HIGHEST)
    consensus_next = gram_solve(gram_matrix, summed.reshape(4, -1)).reshape(summed.shape)
    poly_next = jnp.einsum('fi,ickn->fckn', basis_table, consensus_next, precision=lax.Precision.HIGHEST)
    duals_next = scaled_duals + jones_next - poly_next
    return (jones_next, duals_next, consensus_next)
```

```python
import functools

import jax
import jax.numpy as jnp
import numpy as np
from jax import lax
from jax.experimental import pallas as pl
from jax.experimental.pallas import tpu as pltpu
from jax.sharding import PartitionSpec as P

DIRS = 16
LANES = 128
PENALTY = 40.0
STEP_SIZE = 0.5
MESH = pl.DeviceIdType.MESH
F32 = jnp.float32
BF16 = jnp.bfloat16


def turn_series(count):
    square = np.linspace(0.0, 0.25, 4001)
    root = np.sqrt(square)
    cosine = np.cos(2 * np.pi * root)
    sine = -2 * np.pi * np.sinc(2 * root)
    fits = []
    for target in (cosine, sine):
        fit = np.polynomial.chebyshev.Chebyshev.fit(square, target, count - 1, domain=[0.0, 0.25])
        fits.append([float(c) for c in fit.convert(kind=np.polynomial.Polynomial).coef])
    return fits


COS_SERIES, SIN_SERIES = turn_series(7)


def basis_rows(band_count):
    centre = (2.0 * np.arange(band_count) + 1.0) / band_count - 1.0
    return np.stack(
        [
            np.ones_like(centre),
            centre,
            0.5 * (3.0 * centre**2 - 1.0),
            0.5 * (5.0 * centre**3 - 3.0 * centre),
        ],
        axis=1,
    )


def horner(series, value):
    total = value * series[-1] + series[-2]
    for coefficient in series[-3::-1]:
        total = total * value + coefficient
    return total


def phasor(turns):
    part = turns - jnp.floor(turns + 0.5)
    square = part * part
    return horner(COS_SERIES, square).astype(BF16), (horner(SIN_SERIES, square) * part).astype(BF16)


def packed(value):
    half = value.shape[0] // 2
    rows, cols = half * value.shape[1], value.shape[2]
    return jnp.concatenate([value[:half].reshape(rows, cols), value[half:].reshape(rows, cols)], 1)


def kernel(
    bands,
    blocks,
    vis_ref,
    mask_ref,
    stations_ref,
    dirs_ref,
    flux_ref,
    pol_ref,
    index_ref,
    clusters_ref,
    gains_ref,
    duals_ref,
    cons_ref,
    jones_out,
    duals_out,
    cons_out,
    near_all,
    vis_send,
    vis_recv,
    grad_send,
    grad_recv,
    norm_recv,
    sums_all,
    oh_rank,
    sky_lhs,
    sky_rows,
    sky_cols,
    jones_cols,
    jones_rows,
    place_rows,
    right,
    terms,
    wide,
    mask_sum,
    grads,
    near_ssem,
    near_rsem,
    vis_ssem,
    vis_rsem,
    grad_ssem,
    grad_rsem,
    norm_ssem,
    norm_rsem,
    sums_ssem,
    sums_rsem,
):
    my_band = lax.axis_index("freq")
    my_block = lax.axis_index("stn")
    rows = gains_ref.shape[2]
    total = vis_ref.shape[2]
    comps = clusters_ref.shape[1]
    span = comps // DIRS

    barrier = pltpu.get_barrier_semaphore()
    stn_peers = [lax.rem(my_block + d, blocks) for d in range(1, blocks)]
    freq_peers = [lax.rem(my_band + d, bands) for d in range(1, bands)]
    for peer in stn_peers:
        pl.semaphore_signal(barrier, inc=1, device_id=(my_band, peer), device_id_type=MESH)
    for peer in freq_peers:
        pl.semaphore_signal(barrier, inc=1, device_id=(peer, my_block), device_id_type=MESH)

    def to_blocks(source_of, target, ssem, rsem):
        copies = []
        for at, peer in enumerate(stn_peers):
            copy = pltpu.make_async_remote_copy(
                src_ref=source_of(peer),
                dst_ref=target.at[my_block],
                send_sem=ssem.at[at],
                recv_sem=rsem.at[at],
                device_id=(my_band, peer),
                device_id_type=MESH,
            )
            copy.start()
            copies.append(copy)
        return copies

    gains = gains_ref[...]
    near_all[my_block, 0 : 8 * DIRS] = gains.reshape(8 * DIRS, rows)
    near_all[my_block, 8 * DIRS : 8 * DIRS + 3] = stations_ref[...]
    pl.semaphore_wait(barrier, blocks - 1 + bands - 1)
    near_copies = to_blocks(lambda peer: near_all.at[my_block], near_all, near_ssem, near_rsem)

    mask = mask_ref[...].astype(F32)
    for pair in range(5):
        if pair < 4:
            first, second = vis_ref[2 * pair] * mask, vis_ref[2 * pair + 1] * mask
        else:
            first = second = mask
        both = jnp.concatenate([first, second], 0)
        turned = both.T
        for block in range(blocks):
            vis_send[block, pair] = turned[block * rows : (block + 1) * rows]
        if pair < 4:
            wide[2 * pair] = first
            wide[2 * pair + 1] = second
        else:
            mask_sum[...] = first
    vis_copies = to_blocks(lambda peer: vis_send.at[peer], vis_recv, vis_ssem, vis_rsem)
    vis_recv[my_block] = vis_send[my_block]

    clusters = clusters_ref[...]
    member = (lax.broadcasted_iota(jnp.int32, (DIRS, comps), 0) == clusters).astype(F32)
    chunks = comps // LANES
    stacked = jnp.concatenate([member[:, c * LANES : (c + 1) * LANES] for c in range(chunks)], 0)
    before = (
        lax.broadcasted_iota(jnp.int32, (LANES, LANES), 0)
        < lax.broadcasted_iota(jnp.int32, (LANES, LANES), 1)
    ).astype(BF16)
    prefix = jnp.dot(stacked.astype(BF16), before, preferred_element_type=F32)
    running = jnp.zeros((DIRS, 1), F32)
    rank_iota = lax.broadcasted_iota(jnp.int32, (LANES, LANES), 0).astype(F32)
    for c in range(chunks):
        own = stacked[c * DIRS : (c + 1) * DIRS]
        rank = jnp.sum(own * (prefix[c * DIRS : (c + 1) * DIRS] + running), 0, keepdims=True)
        oh_rank[:, c * LANES : (c + 1) * LANES] = (rank_iota == rank).astype(F32)
        running = running + jnp.sum(own, 1, keepdims=True)
    values = jnp.concatenate(
        [
            dirs_ref[...],
            flux_ref[...],
            pol_ref[...],
            index_ref[...],
            jnp.zeros((2, comps), F32),
        ],
        0,
    )
    for k in range(DIRS):
        sky_lhs[8 * k : 8 * k + 8] = member[k : k + 1] * values
    sky = lax.dot_general(
        sky_lhs[...],
        oh_rank[...],
        (((1,), (1,)), ((), ())),
        precision=lax.Precision.HIGHEST,
        preferred_element_type=F32,
    )
    sky_rows[...] = sky.reshape(DIRS, 8, LANES)
    sky_turned = sky.T
    for k in range(DIRS):
        sky_cols[k] = sky_turned[:, 8 * k : 8 * k + 8]
        jones_cols[k] = gains[:, k, :].T
    zero_rows = jnp.zeros((LANES - span, 2 * total), BF16)
    right[span:LANES] = zero_rows
    right[LANES + span :] = zero_rows
    band_number = my_band.astype(F32)
    ratio = 0.5 + 3.0 * (band_number + 0.5) / bands
    log_ratio = jnp.log(jnp.full((8, LANES), ratio, F32))[0:1]
    own_place = stations_ref[...].T

    for copy in near_copies:
        copy.wait()
    for block in range(blocks):
        cut = slice(block * rows, (block + 1) * rows)
        jones_rows[:, :, cut] = near_all[block, 0 : 8 * DIRS].reshape(8, DIRS, rows)
        place_rows[0:3, cut] = near_all[block, 8 * DIRS : 8 * DIRS + 3]

    def geometry(l_value, m_value, places):
        n_value = jnp.sqrt(1.0 - l_value * l_value - m_value * m_value) - 1.0
        return ratio * (l_value * places[0] + m_value * places[1] + n_value * places[2])

    @pl.loop(0, DIRS)
    def build_terms(k):
        row = sky_rows[k]
        factor = jnp.exp(row[5:6] * log_ratio)
        w_xx = (row[2:3] + row[3:4]) * factor
        w_xy = row[4:5] * factor
        w_yy = (row[2:3] - row[3:4]) * factor
        turns = geometry(row[0:1], row[1:2], [own_place[:, a : a + 1] for a in range(3)])
        own_r, own_i = (value.astype(F32) for value in phasor(turns))
        jones = jones_cols[k]
        weight = ((w_xx, w_xy), (w_xy, w_yy))
        left = []
        for i in range(2):
            j0r, j0i, j1r, j1i = (jones[:, 4 * i + a : 4 * i + a + 1] for a in range(4))
            for j in range(2):
                e_r = j0r * weight[0][j] + j1r * weight[1][j]
                e_i = j0i * weight[0][j] + j1i * weight[1][j]
                left.append(
                    jnp.concatenate(
                        [
                            (own_r * e_r - own_i * e_i).astype(BF16),
                            (own_r * e_i + own_i * e_r).astype(BF16),
                        ],
                        1,
                    )
                )
        col = sky_cols[k][0:span]
        places = [place_rows[a : a + 1, :] for a in range(3)]
        far_r, far_i = phasor(geometry(col[:, 0:1], col[:, 1:2], places))
        right[0:span, 0:total] = far_r
        right[0:span, total:] = -far_i
        right[LANES : LANES + span, 0:total] = far_i
        right[LANES : LANES + span, total:] = far_r
        terms[k] = jnp.dot(
            jnp.concatenate(left, 0), right[...], preferred_element_type=F32
        )

    for copy in vis_copies:
        copy.wait()
    for i in range(2):
        for j in range(2):
            for part in range(2):
                lanes = slice(part * rows, (part + 1) * rows)
                other = jnp.concatenate(
                    [vis_recv[block, 2 * j + i, :, lanes] for block in range(blocks)], 1
                )
                at = 2 * (2 * i + j) + part
                wide[at] = wide[at] + other if part == 0 else wide[at] - other
    mask_sum[...] += jnp.concatenate([vis_recv[block, 4, :, 0:rows] for block in range(blocks)], 1)

    def term_parts(k, row_at):
        out = []
        for entry in range(4):
            cut = pl.ds(pl.multiple_of(entry * rows + row_at * 8, 8), 8)
            out.append((terms[k, cut, 0:total], terms[k, cut, total:]))
        return out

    @pl.loop(0, rows // 8)
    def subtract_model(row_at):
        def add_direction(k, sums):
            t = term_parts(k, row_at)
            sums = list(sums)
            for el in range(2):
                for j in range(2):
                    j_r = jones_rows[2 * (2 * el + j), pl.ds(k, 1), :]
                    j_i = jones_rows[2 * (2 * el + j) + 1, pl.ds(k, 1), :]
                    for i in range(2):
                        t_r, t_i = t[2 * i + j]
                        at = 2 * (2 * i + el)
                        sums[at] = sums[at] + (t_r * j_r + t_i * j_i)
                        sums[at + 1] = sums[at + 1] + (t_i * j_r - t_r * j_i)
            return tuple(sums)

        sums = lax.fori_loop(
            0, DIRS, add_direction, tuple(jnp.zeros((8, total), F32) for _ in range(8))
        )
        cut = pl.ds(pl.multiple_of(row_at * 8, 8), 8)
        both = mask_sum[cut]
        for at in range(8):
            wide[at, cut] = wide[at, cut] - both * sums[at]

    @pl.loop(0, DIRS)
    def gradient(k):
        def add_rows(row_at, sums):
            t = term_parts(k, row_at)
            cut = pl.ds(pl.multiple_of(row_at * 8, 8), 8)
            sums = list(sums)
            for m in range(2):
                for i in range(2):
                    w_r = wide[2 * (2 * m + i), cut]
                    w_i = wide[2 * (2 * m + i) + 1, cut]
                    for j in range(2):
                        t_r, t_i = t[2 * m + j]
                        at = 2 * (2 * i + j)
                        sums[at] = sums[at] + (w_r * t_r + w_i * t_i)
                        sums[at + 1] = sums[at + 1] + (w_r * t_i - w_i * t_r)
            return tuple(sums)

        sums = lax.fori_loop(
            0, rows // 8, add_rows, tuple(jnp.zeros((8, total), F32) for _ in range(8))
        )
        for at in range(8):
            grads[at, pl.ds(k, 1), :] = -jnp.sum(sums[at], 0, keepdims=True)

    for block in range(blocks):
        grad_send[block] = packed(grads[:, :, block * rows : (block + 1) * rows])
    grad_copies = to_blocks(lambda peer: grad_send.at[peer], grad_recv, grad_ssem, grad_rsem)
    centre = (2.0 * band_number + 1.0) / bands - 1.0
    basis = (
        1.0,
        centre,
        0.5 * (3.0 * centre * centre - 1.0),
        0.5 * (5.0 * centre * centre * centre - 3.0 * centre),
    )
    own_jones = packed(gains)
    own_duals = packed(duals_ref[...])
    poly = packed(cons_ref[0])
    for i in range(1, 4):
        poly = poly + basis[i] * packed(cons_ref[i])
    drive = PENALTY / 2.0 * (own_jones - poly + own_duals) + grad_send[my_block]
    for copy in grad_copies:
        copy.wait()
    for peer in stn_peers:
        drive = drive + grad_recv[peer]
    squares = jnp.sum((drive * drive).reshape(-1, 8, 2 * rows), 0)
    norm_recv[my_block] = squares
    norm_copies = to_blocks(lambda peer: norm_recv.at[my_block], norm_recv, norm_ssem, norm_rsem)
    for copy in norm_copies:
        copy.wait()
    squares = norm_recv[0]
    for block in range(1, blocks):
        squares = squares + norm_recv[block]
    mean = jnp.sum(jnp.sum(squares, 0, keepdims=True), 1, keepdims=True) / (8 * DIRS * total)
    step = STEP_SIZE / jnp.sqrt(mean + 1e-06)
    jones_next = own_jones - step * drive
    base = jones_next + own_duals
    sums_all[my_band] = base
    copies = []
    for at, peer in enumerate(freq_peers):
        copy = pltpu.make_async_remote_copy(
            src_ref=sums_all.at[my_band],
            dst_ref=sums_all.at[my_band],
            send_sem=sums_ssem.at[at],
            recv_sem=sums_rsem.at[at],
            device_id=(peer, my_block),
            device_id_type=MESH,
        )
        copy.start()
        copies.append(copy)

    def unpacked(value):
        return [
            value[:, part * rows : (part + 1) * rows].reshape(4, DIRS, rows) for part in range(2)
        ]

    for part, piece in enumerate(unpacked(jones_next)):
        jones_out[4 * part : 4 * part + 4] = piece
    for copy in copies:
        copy.wait()
    table = basis_rows(bands)
    solve = np.linalg.solve(table.T @ table, table.T)
    fitted = None
    for i in range(4):
        value = float(solve[i, 0]) * sums_all[0]
        for band in range(1, bands):
            value = value + float(solve[i, band]) * sums_all[band]
        for part, piece in enumerate(unpacked(value)):
            cons_out[i, 4 * part : 4 * part + 4] = piece
        fitted = value if i == 0 else fitted + basis[i] * value
    for part, piece in enumerate(unpacked(base - fitted)):
        duals_out[4 * part : 4 * part + 4] = piece


def local(
    visibilities,
    flag_mask,
    stations,
    directions,
    intensity,
    polarized,
    spectral,
    clusters,
    jones_gains,
    scaled_duals,
    consensus,
):
    bands = lax.axis_size("freq")
    blocks = lax.axis_size("stn")
    rows, total = flag_mask.shape
    comps = clusters.shape[0]
    vmem = pl.BlockSpec(memory_space=pltpu.VMEM)
    block_sem = pltpu.SemaphoreType.DMA((blocks - 1,))
    outs = pl.pallas_call(
        functools.partial(kernel, bands, blocks),
        out_shape=(
            jax.ShapeDtypeStruct((8, DIRS, rows), F32),
            jax.ShapeDtypeStruct((8, DIRS, rows), F32),
            jax.ShapeDtypeStruct((4, 8, DIRS, rows), F32),
        ),
        in_specs=[vmem] * 11,
        out_specs=(vmem, vmem, vmem),
        scratch_shapes=[
            pltpu.VMEM((blocks, 8 * DIRS + 8, rows), F32),
            pltpu.VMEM((blocks, 5, rows, 2 * rows), F32),
            pltpu.VMEM((blocks, 5, rows, 2 * rows), F32),
            pltpu.VMEM((blocks, 4 * DIRS, 2 * rows), F32),
            pltpu.VMEM((blocks, 4 * DIRS, 2 * rows), F32),
            pltpu.VMEM((blocks, 8, 2 * rows), F32),
            pltpu.VMEM((bands, 4 * DIRS, 2 * rows), F32),
            pltpu.VMEM((LANES, comps), F32),
            pltpu.VMEM((8 * DIRS, comps), F32),
            pltpu.VMEM((DIRS, 8, LANES), F32),
            pltpu.VMEM((DIRS, LANES, 8), F32),
            pltpu.VMEM((DIRS, rows, 8), F32),
            pltpu.VMEM((8, DIRS, total), F32),
            pltpu.VMEM((8, total), F32),
            pltpu.VMEM((2 * LANES, 2 * total), BF16),
            pltpu.VMEM((DIRS, 4 * rows, 2 * total), F32),
            pltpu.VMEM((8, rows, total), F32),
            pltpu.VMEM((rows, total), F32),
            pltpu.VMEM((8, DIRS, total), F32),
        ]
        + [block_sem] * 8
        + [pltpu.SemaphoreType.DMA((bands - 1,))] * 2,
        compiler_params=pltpu.CompilerParams(
            collective_id=0, has_side_effects=True, vmem_limit_bytes=58 * 1024 * 1024
        ),
    )(
        visibilities[0],
        flag_mask,
        stations,
        directions,
        intensity[None],
        polarized,
        spectral[None],
        clusters[None],
        jones_gains[0],
        scaled_duals[0],
        consensus,
    )
    return (outs[0][None], outs[1][None], outs[2])


def solution(mesh):
    placed = (
        P("freq", None, "stn", None),
        P("stn", None),
        P(None, "stn"),
        P(),
        P(),
        P(),
        P(),
        P(),
        P("freq", None, None, "stn"),
        P("freq", None, None, "stn"),
        P(None, None, None, "stn"),
    )
    return jax.shard_map(
        local,
        mesh=mesh,
        in_specs=placed,
        out_specs=(
            P("freq", None, None, "stn"),
            P("freq", None, None, "stn"),
            P(None, None, None, "stn"),
        ),
        check_vma=False,
    )
```

```python
import functools

import jax
import jax.numpy as jnp
import numpy as np
from jax import lax
from jax.experimental import pallas as pl
from jax.experimental.pallas import tpu as pltpu
from jax.sharding import PartitionSpec as P

DIRS = 16
LANES = 128
PENALTY = 40.0
STEP_SIZE = 0.5
MESH = pl.DeviceIdType.MESH
F32 = jnp.float32
BF16 = jnp.bfloat16


def turn_series(count):
    square = np.linspace(0.0, 0.25, 4001)
    root = np.sqrt(square)
    cosine = np.cos(2 * np.pi * root)
    sine = -2 * np.pi * np.sinc(2 * root)
    fits = []
    for target in (cosine, sine):
        fit = np.polynomial.chebyshev.Chebyshev.fit(square, target, count - 1, domain=[0.0, 0.25])
        fits.append([float(c) for c in fit.convert(kind=np.polynomial.Polynomial).coef])
    return fits


COS_SERIES, SIN_SERIES = turn_series(7)


def basis_rows(band_count):
    centre = (2.0 * np.arange(band_count) + 1.0) / band_count - 1.0
    return np.stack(
        [
            np.ones_like(centre),
            centre,
            0.5 * (3.0 * centre**2 - 1.0),
            0.5 * (5.0 * centre**3 - 3.0 * centre),
        ],
        axis=1,
    )


def horner(series, value):
    total = value * series[-1] + series[-2]
    for coefficient in series[-3::-1]:
        total = total * value + coefficient
    return total


def phasor(turns):
    part = turns - jnp.floor(turns + 0.5)
    square = part * part
    return horner(COS_SERIES, square).astype(BF16), (horner(SIN_SERIES, square) * part).astype(BF16)


def packed(value):
    half = value.shape[0] // 2
    rows, cols = half * value.shape[1], value.shape[2]
    return jnp.concatenate([value[:half].reshape(rows, cols), value[half:].reshape(rows, cols)], 1)


def kernel(
    bands,
    blocks,
    vis_ref,
    mask_ref,
    stations_ref,
    dirs_ref,
    flux_ref,
    pol_ref,
    index_ref,
    clusters_ref,
    gains_ref,
    duals_ref,
    cons_ref,
    result,
    near_all,
    vis_send,
    vis_recv,
    base_all,
    drive_all,
    norm_all,
    step_all,
    oh_rank,
    sky_lhs,
    sky_rows,
    sky_cols,
    jones_cols,
    jones_rows,
    place_rows,
    left_even,
    left_odd,
    right_even,
    right_odd,
    coh,
    far_terms,
    wide,
    mask_sum,
    grad_cols,
    near_ssem,
    near_rsem,
    vis_ssem,
    vis_rsem,
    norm_ssem,
    norm_rsem,
    base_ssem,
    base_rsem,
    drive_ssem,
    drive_rsem,
    step_ssem,
    step_rsem,
):
    my_band = lax.axis_index("freq")
    my_block = lax.axis_index("stn")
    rows = gains_ref.shape[2]
    total = vis_ref.shape[2]
    comps = clusters_ref.shape[0]
    span = comps // DIRS

    barrier = pltpu.get_barrier_semaphore()
    stn_peers = [lax.rem(my_block + d, blocks) for d in range(1, blocks)]
    freq_peers = [lax.rem(my_band + d, bands) for d in range(1, bands)]
    for peer in stn_peers:
        pl.semaphore_signal(barrier, inc=1, device_id=(my_band, peer), device_id_type=MESH)
    for peer in freq_peers:
        pl.semaphore_signal(barrier, inc=1, device_id=(peer, my_block), device_id_type=MESH)

    def send(source, target, ssem, rsem, at, device):
        copy = pltpu.make_async_remote_copy(
            src_ref=source,
            dst_ref=target,
            send_sem=ssem.at[at],
            recv_sem=rsem.at[at],
            device_id=device,
            device_id_type=MESH,
        )
        copy.start()
        return copy

    def to_blocks(source_of, target, ssem, rsem):
        return [
            send(source_of(peer), target.at[my_block], ssem, rsem, at, (my_band, peer))
            for at, peer in enumerate(stn_peers)
        ]

    def to_bands(target, ssem, rsem):
        own = target.at[my_band]
        return [
            send(own, own, ssem, rsem, at, (peer, my_block)) for at, peer in enumerate(freq_peers)
        ]

    gains = gains_ref[...]
    near_all[my_block, 0 : 8 * DIRS] = gains.reshape(8 * DIRS, rows)
    near_all[my_block, 8 * DIRS : 8 * DIRS + 3] = stations_ref[...]
    own_jones = packed(gains)
    base_all[my_band] = own_jones + packed(duals_ref[...])

    mask = mask_ref[...].astype(F32)
    for pair in range(5):
        if pair < 4:
            first, second = vis_ref[2 * pair] * mask, vis_ref[2 * pair + 1] * mask
        else:
            first = second = mask
        turned = jnp.concatenate([first, second], 0).T
        for block in range(blocks):
            vis_send[block, pair] = turned[block * rows : (block + 1) * rows]
        if pair < 4:
            wide[2 * pair] = first
            wide[2 * pair + 1] = second
        else:
            mask_sum[...] = first
    pl.semaphore_wait(barrier, blocks - 1 + bands - 1)
    near_copies = to_blocks(lambda peer: near_all.at[my_block], near_all, near_ssem, near_rsem)
    vis_copies = to_blocks(lambda peer: vis_send.at[peer], vis_recv, vis_ssem, vis_rsem)
    base_copies = to_bands(base_all, base_ssem, base_rsem)
    vis_recv[my_block] = vis_send[my_block]

    clusters = clusters_ref[...].reshape(1, comps)
    member = (lax.broadcasted_iota(jnp.int32, (DIRS, comps), 0) == clusters).astype(F32)
    chunks = comps // LANES
    stacked = jnp.concatenate([member[:, c * LANES : (c + 1) * LANES] for c in range(chunks)], 0)
    before = (
        lax.broadcasted_iota(jnp.int32, (LANES, LANES), 0)
        < lax.broadcasted_iota(jnp.int32, (LANES, LANES), 1)
    ).astype(BF16)
    prefix = jnp.dot(stacked.astype(BF16), before, preferred_element_type=F32)
    running = jnp.zeros((DIRS, 1), F32)
    rank_iota = lax.broadcasted_iota(jnp.int32, (LANES, LANES), 0).astype(F32)
    for c in range(chunks):
        own = stacked[c * DIRS : (c + 1) * DIRS]
        rank = jnp.sum(own * (prefix[c * DIRS : (c + 1) * DIRS] + running), 0, keepdims=True)
        oh_rank[:, c * LANES : (c + 1) * LANES] = (rank_iota == rank).astype(BF16)
        running = running + jnp.sum(own, 1, keepdims=True)
    values = jnp.concatenate(
        [
            dirs_ref[...],
            flux_ref[...].reshape(1, comps),
            pol_ref[...],
            index_ref[...].reshape(1, comps),
            jnp.zeros((2, comps), F32),
        ],
        0,
    )
    high = values.astype(BF16).astype(F32)
    middle = (values - high).astype(BF16).astype(F32)
    low = values - high - middle
    parts = jnp.concatenate([high, middle, low, jnp.zeros_like(low)], 0)
    for k in range(DIRS):
        sky_lhs[32 * k : 32 * k + 32] = (member[k : k + 1] * parts).astype(BF16)
    sky = lax.dot_general(
        sky_lhs[...], oh_rank[...], (((1,), (1,)), ((), ())), preferred_element_type=F32
    ).reshape(DIRS, 4, 8, LANES)
    sky = (sky[:, 2] + sky[:, 1]) + sky[:, 0]
    sky_rows[...] = sky
    sky_turned = sky.reshape(DIRS * 8, LANES).T
    for k in range(DIRS):
        sky_cols[k] = sky_turned[:, 8 * k : 8 * k + 8]
        jones_cols[k] = gains[:, k, :].T
    zero_rows = jnp.zeros((LANES - span, 2 * total), BF16)
    for right in (right_even, right_odd):
        right[span:LANES] = zero_rows
        right[LANES + span :] = zero_rows
    band_number = my_band.astype(F32)
    ratio = 0.5 + 3.0 * (band_number + 0.5) / bands
    log_ratio = jnp.log(jnp.full((8, LANES), ratio, F32))[0:1]
    own_place = stations_ref[...].T

    for copy in near_copies:
        copy.wait()
    for block in range(blocks):
        cut = slice(block * rows, (block + 1) * rows)
        jones_rows[:, :, cut] = near_all[block, 0 : 8 * DIRS].reshape(8, DIRS, rows)
        place_rows[0:3, cut] = near_all[block, 8 * DIRS : 8 * DIRS + 3]

    def geometry(l_value, m_value, places):
        n_value = jnp.sqrt(1.0 - l_value * l_value - m_value * m_value) - 1.0
        return ratio * (l_value * places[0] + m_value * places[1] + n_value * places[2])

    def build(k, left, right):
        row = sky_rows[k]
        factor = jnp.exp(row[5:6] * log_ratio)
        weights = (
            (row[2:3] + row[3:4]) * factor,
            row[4:5] * factor,
            (row[2:3] - row[3:4]) * factor,
        )
        turns = geometry(row[0:1], row[1:2], [own_place[:, a : a + 1] for a in range(3)])
        own_r, own_i = (value.astype(F32) for value in phasor(turns))
        for at, weight in enumerate(weights):
            left[at * rows : (at + 1) * rows, 0:LANES] = (own_r * weight).astype(BF16)
            left[at * rows : (at + 1) * rows, LANES:] = (own_i * weight).astype(BF16)
        col = sky_cols[k][0:span]
        places = [place_rows[a : a + 1, :] for a in range(3)]
        far_r, far_i = phasor(geometry(col[:, 0:1], col[:, 1:2], places))
        right[0:span, 0:total] = far_r
        right[0:span, total:] = -far_i
        right[LANES : LANES + span, 0:total] = far_i
        right[LANES : LANES + span, total:] = far_r

    def multiply(k, left, right):
        coh[k] = jnp.dot(left[...], right[...], preferred_element_type=F32)

    build(0, left_even, right_even)

    @pl.loop(0, DIRS // 2)
    def coherencies(at):
        build(2 * at + 1, left_odd, right_odd)
        multiply(2 * at, left_even, right_even)
        build(jnp.minimum(2 * at + 2, DIRS - 1), left_even, right_even)
        multiply(2 * at + 1, left_odd, right_odd)

    for copy in vis_copies:
        copy.wait()
    for i in range(2):
        for j in range(2):
            for part in range(2):
                lanes = slice(part * rows, (part + 1) * rows)
                other = jnp.concatenate(
                    [vis_recv[block, 2 * j + i, :, lanes] for block in range(blocks)], 1
                )
                at = 2 * (2 * i + j) + part
                wide[at] = wide[at] + other if part == 0 else wide[at] - other
    mask_sum[...] += jnp.concatenate([vis_recv[block, 4, :, 0:rows] for block in range(blocks)], 1)
    lane = lax.broadcasted_iota(jnp.int32, (8, 8 * DIRS), 1)

    @pl.loop(0, rows // 8)
    def gradient(row_at):
        cut = pl.ds(pl.multiple_of(row_at * 8, 8), 8)

        def add_model(k, sums):
            entries = []
            for at in range(3):
                rows_at = pl.ds(pl.multiple_of(at * rows + row_at * 8, 8), 8)
                entries.append((coh[k, rows_at, 0:total], coh[k, rows_at, total:]))
            matrix = ((entries[0], entries[1]), (entries[1], entries[2]))
            near = jones_cols[k, cut, :]
            sums = list(sums)
            for el in range(2):
                far = [
                    tuple(jones_rows[4 * el + 2 * n + a, pl.ds(k, 1), :] for a in range(2))
                    for n in range(2)
                ]
                for m in range(2):
                    (a_r, a_i), (b_r, b_i) = matrix[m]
                    (c_r, c_i), (d_r, d_i) = far
                    y_r = (a_r * c_r + a_i * c_i) + (b_r * d_r + b_i * d_i)
                    y_i = (a_i * c_r - a_r * c_i) + (b_i * d_r - b_r * d_i)
                    far_terms[k, 4 * m + 2 * el] = y_r
                    far_terms[k, 4 * m + 2 * el + 1] = y_i
                    for i in range(2):
                        p_r = near[:, 4 * i + 2 * m : 4 * i + 2 * m + 1]
                        p_i = near[:, 4 * i + 2 * m + 1 : 4 * i + 2 * m + 2]
                        at = 4 * i + 2 * el
                        sums[at] = sums[at] + (p_r * y_r - p_i * y_i)
                        sums[at + 1] = sums[at + 1] + (p_r * y_i + p_i * y_r)
            return tuple(sums)

        sums = lax.fori_loop(
            0, DIRS, add_model, tuple(jnp.zeros((8, total), F32) for _ in range(8)), unroll=2
        )
        both = mask_sum[cut]
        w = [wide[at, cut] - both * sums[at] for at in range(8)]

        def add_gradient(k, columns):
            y = [far_terms[k, at] for at in range(8)]
            for i in range(2):
                for j in range(2):
                    real = imag = None
                    for m in range(2):
                        w_r, w_i = w[4 * i + 2 * m], w[4 * i + 2 * m + 1]
                        y_r, y_i = y[4 * j + 2 * m], y[4 * j + 2 * m + 1]
                        one, two = w_r * y_r + w_i * y_i, w_i * y_r - w_r * y_i
                        real, imag = (one, two) if m == 0 else (real + one, imag + two)
                    for part, member_sum in enumerate((real, imag)):
                        place = (4 * i + 2 * j + part) * DIRS + k
                        summed = jnp.sum(member_sum, 1, keepdims=True)
                        columns = jnp.where(lane == place, summed, columns)
            return columns

        grad_cols[cut] = lax.fori_loop(
            0, DIRS, add_gradient, jnp.zeros((8, 8 * DIRS), F32), unroll=4
        )

    centre = (2.0 * band_number + 1.0) / bands - 1.0
    basis = (
        1.0,
        centre,
        0.5 * (3.0 * centre * centre - 1.0),
        0.5 * (5.0 * centre * centre * centre - 3.0 * centre),
    )
    poly = packed(cons_ref[0])
    for i in range(1, 4):
        poly = poly + basis[i] * packed(cons_ref[i])
    base = base_all[my_band]
    turned = grad_cols[...].T
    grads = jnp.concatenate([turned[0 : 4 * DIRS], turned[4 * DIRS :]], 1)
    drive = PENALTY / 2.0 * (base - poly) - grads
    drive_all[my_band] = drive
    norm_all[my_block] = jnp.sum((drive * drive).reshape(-1, 8, 2 * rows), 0)
    norm_copies = to_blocks(lambda peer: norm_all.at[my_block], norm_all, norm_ssem, norm_rsem)
    drive_copies = to_bands(drive_all, drive_ssem, drive_rsem)
    for copy in norm_copies:
        copy.wait()
    squares = norm_all[0]
    for block in range(1, blocks):
        squares = squares + norm_all[block]
    mean = jnp.sum(jnp.sum(squares, 0, keepdims=True), 1, keepdims=True) / (8 * DIRS * total)
    step_all[my_band] = jnp.broadcast_to(STEP_SIZE / jnp.sqrt(mean + 1e-06), (8, 2 * rows))
    step_copies = to_bands(step_all, step_ssem, step_rsem)
    result[0] = own_jones - step_all[my_band, 0:1] * drive
    for copy in base_copies + drive_copies + step_copies:
        copy.wait()
    sums = [
        base_all[band] - step_all[band, 0:1] * drive_all[band] for band in range(bands)
    ]
    table = basis_rows(bands)
    solve = np.linalg.solve(table.T @ table, table.T)
    fitted = None
    for i in range(4):
        value = float(solve[i, 0]) * sums[0]
        for band in range(1, bands):
            value = value + float(solve[i, band]) * sums[band]
        result[2 + i] = value
        fitted = value if i == 0 else fitted + basis[i] * value
    result[1] = base - step_all[my_band, 0:1] * drive - fitted


def spread(result, jones_out, duals_out, cons_out):
    rows = jones_out.shape[2]
    for part in range(2):
        lanes = slice(part * rows, (part + 1) * rows)
        cut = slice(4 * part, 4 * part + 4)
        jones_out[cut] = result[0, :, lanes].reshape(4, DIRS, rows)
        duals_out[cut] = result[1, :, lanes].reshape(4, DIRS, rows)
        for i in range(4):
            cons_out[i, cut] = result[2 + i, :, lanes].reshape(4, DIRS, rows)


def local(
    visibilities,
    flag_mask,
    stations,
    directions,
    intensity,
    polarized,
    spectral,
    clusters,
    jones_gains,
    scaled_duals,
    consensus,
):
    bands = lax.axis_size("freq")
    blocks = lax.axis_size("stn")
    rows, total = flag_mask.shape
    comps = clusters.shape[0]
    vmem = pl.BlockSpec(memory_space=pltpu.VMEM)
    block_sem = pltpu.SemaphoreType.DMA((blocks - 1,))
    band_sem = pltpu.SemaphoreType.DMA((bands - 1,))
    result = pl.pallas_call(
        functools.partial(kernel, bands, blocks),
        out_shape=jax.ShapeDtypeStruct((6, 4 * DIRS, 2 * rows), F32),
        in_specs=[vmem] * 11,
        out_specs=vmem,
        scratch_shapes=[
            pltpu.VMEM((blocks, 8 * DIRS + 8, rows), F32),
            pltpu.VMEM((blocks, 5, rows, 2 * rows), F32),
            pltpu.VMEM((blocks, 5, rows, 2 * rows), F32),
            pltpu.VMEM((bands, 4 * DIRS, 2 * rows), F32),
            pltpu.VMEM((bands, 4 * DIRS, 2 * rows), F32),
            pltpu.VMEM((blocks, 8, 2 * rows), F32),
            pltpu.VMEM((bands, 8, 2 * rows), F32),
            pltpu.VMEM((LANES, comps), BF16),
            pltpu.VMEM((32 * DIRS, comps), BF16),
            pltpu.VMEM((DIRS, 8, LANES), F32),
            pltpu.VMEM((DIRS, LANES, 8), F32),
            pltpu.VMEM((DIRS, rows, 8), F32),
            pltpu.VMEM((8, DIRS, total), F32),
            pltpu.VMEM((8, total), F32),
            pltpu.VMEM((3 * rows, 2 * LANES), BF16),
            pltpu.VMEM((3 * rows, 2 * LANES), BF16),
            pltpu.VMEM((2 * LANES, 2 * total), BF16),
            pltpu.VMEM((2 * LANES, 2 * total), BF16),
            pltpu.VMEM((DIRS, 3 * rows, 2 * total), F32),
            pltpu.VMEM((DIRS, 8, 8, total), F32),
            pltpu.VMEM((8, rows, total), F32),
            pltpu.VMEM((rows, total), F32),
            pltpu.VMEM((rows, 8 * DIRS), F32),
        ]
        + [block_sem] * 6
        + [band_sem] * 6,
        compiler_params=pltpu.CompilerParams(
            collective_id=0, has_side_effects=True, vmem_limit_bytes=58 * 1024 * 1024
        ),
    )(
        visibilities[0],
        flag_mask,
        stations,
        directions,
        intensity,
        polarized,
        spectral,
        clusters,
        jones_gains[0],
        scaled_duals[0],
        consensus,
    )
    outs = pl.pallas_call(
        spread,
        out_shape=(
            jax.ShapeDtypeStruct((8, DIRS, rows), F32),
            jax.ShapeDtypeStruct((8, DIRS, rows), F32),
            jax.ShapeDtypeStruct((4, 8, DIRS, rows), F32),
        ),
        in_specs=[vmem],
        out_specs=(vmem, vmem, vmem),
    )(result)
    return (outs[0][None], outs[1][None], outs[2])


def solution(mesh):
    placed = (
        P("freq", None, "stn", None),
        P("stn", None),
        P(None, "stn"),
        P(),
        P(),
        P(),
        P(),
        P(),
        P("freq", None, None, "stn"),
        P("freq", None, None, "stn"),
        P(None, None, None, "stn"),
    )
    return jax.shard_map(
        local,
        mesh=mesh,
        in_specs=placed,
        out_specs=(
            P("freq", None, None, "stn"),
            P("freq", None, None, "stn"),
            P(None, None, None, "stn"),
        ),
        check_vma=False,
    )
```

```python
import functools

import jax
import jax.numpy as jnp
import numpy as np
from jax import lax
from jax.experimental import pallas as pl
from jax.experimental.pallas import tpu as pltpu
from jax.sharding import PartitionSpec as P

DIRS = 16
LANES = 128
BF16_ROWS = 16
PENALTY = 40.0
STEP_SIZE = 0.5
MESH = pl.DeviceIdType.MESH
F32 = jnp.float32
BF16 = jnp.bfloat16


def turn_series(count):
    square = np.linspace(0.0, 0.25, 4001)
    root = np.sqrt(square)
    cosine = np.cos(2 * np.pi * root)
    sine = -2 * np.pi * np.sinc(2 * root)
    fits = []
    for target in (cosine, sine):
        fit = np.polynomial.chebyshev.Chebyshev.fit(square, target, count - 1, domain=[0.0, 0.25])
        fits.append([float(c) for c in fit.convert(kind=np.polynomial.Polynomial).coef])
    return fits


COS_SERIES, SIN_SERIES = turn_series(7)


def basis_rows(band_count):
    centre = (2.0 * np.arange(band_count) + 1.0) / band_count - 1.0
    return np.stack(
        [
            np.ones_like(centre),
            centre,
            0.5 * (3.0 * centre**2 - 1.0),
            0.5 * (5.0 * centre**3 - 3.0 * centre),
        ],
        axis=1,
    )


def horner(series, value):
    total = value * series[-1] + series[-2]
    for coefficient in series[-3::-1]:
        total = total * value + coefficient
    return total


def phasor(turns):
    part = turns - jnp.floor(turns + 0.5)
    square = part * part
    return horner(COS_SERIES, square).astype(BF16), (horner(SIN_SERIES, square) * part).astype(BF16)


def packed(value):
    half = value.shape[0] // 2
    rows, cols = half * value.shape[1], value.shape[2]
    return jnp.concatenate([value[:half].reshape(rows, cols), value[half:].reshape(rows, cols)], 1)


def kernel(
    bands,
    blocks,
    vis_ref,
    mask_ref,
    stations_ref,
    dirs_ref,
    flux_ref,
    pol_ref,
    index_ref,
    clusters_ref,
    gains_ref,
    duals_ref,
    cons_ref,
    result,
    near_all,
    place_all,
    vis_send,
    vis_recv,
    base_all,
    drive_all,
    norm_all,
    step_all,
    oh_rank,
    sky_lhs,
    sky_rows,
    sky_cols,
    jones_cols,
    jones_rows,
    jones_far,
    place_rows,
    left_even,
    left_odd,
    right_even,
    right_odd,
    coh,
    far_terms,
    wide,
    mask_sum,
    grad_cols,
    near_ssem,
    near_rsem,
    place_ssem,
    place_rsem,
    vis_ssem,
    vis_rsem,
    norm_ssem,
    norm_rsem,
    base_ssem,
    base_rsem,
    drive_ssem,
    drive_rsem,
    step_ssem,
    step_rsem,
):
    my_band = lax.axis_index("freq")
    my_block = lax.axis_index("stn")
    rows = gains_ref.shape[2]
    total = vis_ref.shape[2]
    comps = clusters_ref.shape[0]
    span = comps // DIRS

    barrier = pltpu.get_barrier_semaphore()
    stn_peers = [lax.rem(my_block + d, blocks) for d in range(1, blocks)]
    freq_peers = [lax.rem(my_band + d, bands) for d in range(1, bands)]
    for peer in stn_peers:
        pl.semaphore_signal(barrier, inc=1, device_id=(my_band, peer), device_id_type=MESH)
    for peer in freq_peers:
        pl.semaphore_signal(barrier, inc=1, device_id=(peer, my_block), device_id_type=MESH)

    def send(source, target, ssem, rsem, at, device):
        copy = pltpu.make_async_remote_copy(
            src_ref=source,
            dst_ref=target,
            send_sem=ssem.at[at],
            recv_sem=rsem.at[at],
            device_id=device,
            device_id_type=MESH,
        )
        copy.start()
        return copy

    def to_blocks(source_of, target, ssem, rsem):
        return [
            send(source_of(peer), target.at[my_block], ssem, rsem, at, (my_band, peer))
            for at, peer in enumerate(stn_peers)
        ]

    def to_bands(target, ssem, rsem):
        own = target.at[my_band]
        return [
            send(own, own, ssem, rsem, at, (peer, my_block)) for at, peer in enumerate(freq_peers)
        ]

    gains = gains_ref[...]
    own_jones = packed(gains)
    near_all[my_block] = own_jones
    place_all[my_block] = jnp.zeros((8, 2 * rows), F32)
    place_all[my_block, 0:3, 0:rows] = stations_ref[...]
    base_all[my_band] = own_jones + packed(duals_ref[...])

    mask = mask_ref[...].astype(F32)
    for pair in range(5):
        if pair < 4:
            first, second = vis_ref[2 * pair] * mask, vis_ref[2 * pair + 1] * mask
        else:
            first = second = mask
        turned = jnp.concatenate([first, second], 0).T.astype(BF16)
        for block in range(blocks):
            vis_send[block, pair] = turned[block * rows : (block + 1) * rows]
        if pair < 4:
            wide[2 * pair] = first
            wide[2 * pair + 1] = second
        else:
            mask_sum[...] = first
    pl.semaphore_wait(barrier, blocks - 1 + bands - 1)
    place_copies = to_blocks(
        lambda peer: place_all.at[my_block], place_all, place_ssem, place_rsem
    )
    near_copies = to_blocks(lambda peer: near_all.at[my_block], near_all, near_ssem, near_rsem)
    vis_copies = to_blocks(lambda peer: vis_send.at[peer], vis_recv, vis_ssem, vis_rsem)
    base_copies = to_bands(base_all, base_ssem, base_rsem)
    vis_recv[my_block] = vis_send[my_block]

    clusters = clusters_ref[...].reshape(1, comps)
    member = (lax.broadcasted_iota(jnp.int32, (DIRS, comps), 0) == clusters).astype(F32)
    chunks = comps // LANES
    stacked = jnp.concatenate([member[:, c * LANES : (c + 1) * LANES] for c in range(chunks)], 0)
    before = (
        lax.broadcasted_iota(jnp.int32, (LANES, LANES), 0)
        < lax.broadcasted_iota(jnp.int32, (LANES, LANES), 1)
    ).astype(BF16)
    prefix = jnp.dot(stacked.astype(BF16), before, preferred_element_type=F32)
    running = jnp.zeros((DIRS, 1), F32)
    rank_iota = lax.broadcasted_iota(jnp.int32, (LANES, LANES), 0).astype(F32)
    for c in range(chunks):
        own = stacked[c * DIRS : (c + 1) * DIRS]
        rank = jnp.sum(own * (prefix[c * DIRS : (c + 1) * DIRS] + running), 0, keepdims=True)
        oh_rank[:, c * LANES : (c + 1) * LANES] = (rank_iota == rank).astype(BF16)
        running = running + jnp.sum(own, 1, keepdims=True)
    values = jnp.concatenate(
        [
            dirs_ref[...],
            flux_ref[...].reshape(1, comps),
            pol_ref[...],
            index_ref[...].reshape(1, comps),
            jnp.zeros((2, comps), F32),
        ],
        0,
    )
    high = values.astype(BF16).astype(F32)
    middle = (values - high).astype(BF16).astype(F32)
    low = values - high - middle
    parts = jnp.concatenate([high, middle, low, jnp.zeros_like(low)], 0)
    for k in range(DIRS):
        sky_lhs[32 * k : 32 * k + 32] = (member[k : k + 1] * parts).astype(BF16)
    sky = lax.dot_general(
        sky_lhs[...], oh_rank[...], (((1,), (1,)), ((), ())), preferred_element_type=F32
    ).reshape(DIRS, 4, 8, LANES)
    sky = (sky[:, 2] + sky[:, 1]) + sky[:, 0]
    sky_rows[...] = sky
    sky_turned = sky.reshape(DIRS * 8, LANES).T
    for k in range(DIRS):
        sky_cols[k] = sky_turned[:, 8 * k : 8 * k + 8]
        jones_cols[k] = gains[:, k, :].T
    zero_rows = jnp.zeros((LANES - span, 2 * total), BF16)
    for right in (right_even, right_odd):
        right[span:LANES] = zero_rows
        right[LANES + span :] = zero_rows
    band_number = my_band.astype(F32)
    ratio = 0.5 + 3.0 * (band_number + 0.5) / bands
    log_ratio = jnp.log(jnp.full((8, LANES), ratio, F32))[0:1]
    own_place = stations_ref[...].T

    for copy in place_copies:
        copy.wait()
    for block in range(blocks):
        place_rows[:, block * rows : (block + 1) * rows] = place_all[block, :, 0:rows]

    def n_less(l_value, m_value):
        return jnp.sqrt(1.0 - l_value * l_value - m_value * m_value) - 1.0

    def geometry(l_value, m_value, n_value, places):
        return ratio * (l_value * places[0] + m_value * places[1] + n_value * places[2])

    def build(k, left, right):
        row = sky_rows[k]
        factor = jnp.exp(row[5:6] * log_ratio)
        weights = (
            (row[2:3] + row[3:4]) * factor,
            row[4:5] * factor,
            (row[2:3] - row[3:4]) * factor,
        )
        step = 2 * BF16_ROWS
        for low in range(0, rows, step):
            places = [own_place[low : low + step, a : a + 1] for a in range(3)]
            turns = geometry(row[0:1], row[1:2], n_less(row[0:1], row[1:2]), places)
            own_r, own_i = (value.astype(F32) for value in phasor(turns))
            for at, weight in enumerate(weights):
                cut = slice(at * rows + low, at * rows + low + step)
                left[cut, 0:LANES] = (own_r * weight).astype(BF16)
                left[cut, LANES:] = (own_i * weight).astype(BF16)
        places = [place_rows[a : a + 1, :] for a in range(3)]
        low = 0
        while low < span:
            high = min(low + step, span)
            l_col, m_col = sky_cols[k, low:high, 0:1], sky_cols[k, low:high, 1:2]
            n_col = n_less(l_col, m_col)
            for tile in range(0, total, LANES):
                lanes = slice(tile, tile + LANES)
                turns = geometry(l_col, m_col, n_col, [place[:, lanes] for place in places])
                far_r, far_i = phasor(turns)
                right[low:high, lanes] = far_r
                right[low:high, total + tile : total + tile + LANES] = -far_i
                right[LANES + low : LANES + high, lanes] = far_i
                right[LANES + low : LANES + high, total + tile : total + tile + LANES] = far_r
            low = high

    def multiply(k, left, right):
        coh[k] = jnp.dot(left[...], right[...], preferred_element_type=F32)

    build(0, left_even, right_even)

    @pl.loop(0, DIRS // 2 - 1)
    def coherencies(at):
        build(2 * at + 1, left_odd, right_odd)
        multiply(2 * at, left_even, right_even)
        build(2 * at + 2, left_even, right_even)
        multiply(2 * at + 1, left_odd, right_odd)

    build(DIRS - 1, left_odd, right_odd)
    multiply(DIRS - 2, left_even, right_even)
    multiply(DIRS - 1, left_odd, right_odd)

    for copy in near_copies:
        copy.wait()
    for block in range(blocks):
        cut = slice(block * rows, (block + 1) * rows)
        near = near_all[block]
        jones_rows[0:4, :, cut] = near[:, 0:rows].reshape(4, DIRS, rows)
        jones_rows[4:8, :, cut] = near[:, rows:].reshape(4, DIRS, rows)
    for k in range(DIRS):
        for at in range(8):
            jones_far[k, at] = jnp.broadcast_to(jones_rows[at, k : k + 1, :], (8, total))
    for copy in vis_copies:
        copy.wait()
    for i in range(2):
        for j in range(2):
            for part in range(2):
                lanes = slice(part * rows, (part + 1) * rows)
                other = jnp.concatenate(
                    [vis_recv[block, 2 * j + i, :, lanes].astype(F32) for block in range(blocks)],
                    1,
                )
                at = 2 * (2 * i + j) + part
                wide[at] = wide[at] + other if part == 0 else wide[at] - other
    mask_sum[...] += jnp.concatenate(
        [vis_recv[block, 4, :, 0:rows].astype(F32) for block in range(blocks)], 1
    )
    lane = lax.broadcasted_iota(jnp.int32, (8, 8 * DIRS), 1)

    @pl.loop(0, rows // 8)
    def gradient(row_at):
        cut = pl.ds(pl.multiple_of(row_at * 8, 8), 8)

        tiles = [slice(tile, tile + LANES) for tile in range(0, total, LANES)]

        def add_model(k, sums):
            near = jones_cols[k, cut, :]
            near = [jnp.broadcast_to(near[:, at : at + 1], (8, LANES)) for at in range(8)]
            done = []
            for tile, lanes in enumerate(tiles):
                far_lanes = slice(total + tile * LANES, total + (tile + 1) * LANES)
                entries = []
                for at in range(3):
                    rows_at = pl.ds(pl.multiple_of(at * rows + row_at * 8, 8), 8)
                    entries.append((coh[k, rows_at, lanes], coh[k, rows_at, far_lanes]))
                matrix = ((entries[0], entries[1]), (entries[1], entries[2]))
                own = list(sums[8 * tile : 8 * tile + 8])
                for el in range(2):
                    c_r, c_i, d_r, d_i = (jones_far[k, 4 * el + a, :, lanes] for a in range(4))
                    for m in range(2):
                        (a_r, a_i), (b_r, b_i) = matrix[m]
                        y_r = (a_r * c_r + a_i * c_i) + (b_r * d_r + b_i * d_i)
                        y_i = (a_i * c_r - a_r * c_i) + (b_i * d_r - b_r * d_i)
                        far_terms[k, 4 * m + 2 * el, :, lanes] = y_r
                        far_terms[k, 4 * m + 2 * el + 1, :, lanes] = y_i
                        for i in range(2):
                            p_r, p_i = near[4 * i + 2 * m], near[4 * i + 2 * m + 1]
                            at = 4 * i + 2 * el
                            own[at] = own[at] + (p_r * y_r - p_i * y_i)
                            own[at + 1] = own[at + 1] + (p_r * y_i + p_i * y_r)
                done += own
            return tuple(done)

        sums = lax.fori_loop(
            0,
            DIRS,
            add_model,
            tuple(jnp.zeros((8, LANES), F32) for _ in range(8 * len(tiles))),
            unroll=2,
        )
        w = [
            [
                wide[at, cut, lanes] - mask_sum[cut, lanes] * sums[8 * tile + at]
                for at in range(8)
            ]
            for tile, lanes in enumerate(tiles)
        ]

        def add_gradient(k, columns):
            totals = [None] * 8
            for tile, lanes in enumerate(tiles):
                y = [far_terms[k, at, :, lanes] for at in range(8)]
                for i in range(2):
                    for j in range(2):
                        at = 4 * i + 2 * j
                        for m in range(2):
                            w_r, w_i = w[tile][4 * i + 2 * m], w[tile][4 * i + 2 * m + 1]
                            y_r, y_i = y[4 * j + 2 * m], y[4 * j + 2 * m + 1]
                            both = (w_r * y_r + w_i * y_i, w_i * y_r - w_r * y_i)
                            for part in range(2):
                                old = totals[at + part]
                                totals[at + part] = both[part] if old is None else old + both[part]
            for at in range(8):
                summed = jnp.sum(totals[at], 1, keepdims=True)
                columns = jnp.where(lane == at * DIRS + k, summed, columns)
            return columns

        grad_cols[cut] = lax.fori_loop(
            0, DIRS, add_gradient, jnp.zeros((8, 8 * DIRS), F32), unroll=4
        )

    centre = (2.0 * band_number + 1.0) / bands - 1.0
    basis = (
        1.0,
        centre,
        0.5 * (3.0 * centre * centre - 1.0),
        0.5 * (5.0 * centre * centre * centre - 3.0 * centre),
    )
    poly = packed(cons_ref[0])
    for i in range(1, 4):
        poly = poly + basis[i] * packed(cons_ref[i])
    base = base_all[my_band]
    turned = grad_cols[...].T
    grads = jnp.concatenate([turned[0 : 4 * DIRS], turned[4 * DIRS :]], 1)
    drive = PENALTY / 2.0 * (base - poly) - grads
    drive_all[my_band] = drive
    norm_all[my_block] = jnp.sum((drive * drive).reshape(-1, 8, 2 * rows), 0)
    norm_copies = to_blocks(lambda peer: norm_all.at[my_block], norm_all, norm_ssem, norm_rsem)
    drive_copies = to_bands(drive_all, drive_ssem, drive_rsem)
    for copy in norm_copies:
        copy.wait()
    squares = norm_all[0]
    for block in range(1, blocks):
        squares = squares + norm_all[block]
    mean = jnp.sum(jnp.sum(squares, 0, keepdims=True), 1, keepdims=True) / (8 * DIRS * total)
    step_all[my_band] = jnp.broadcast_to(STEP_SIZE / jnp.sqrt(mean + 1e-06), (8, 2 * rows))
    step_copies = to_bands(step_all, step_ssem, step_rsem)
    result[0] = own_jones - step_all[my_band, 0:1] * drive
    for copy in base_copies + drive_copies + step_copies:
        copy.wait()
    sums = [
        base_all[band] - step_all[band, 0:1] * drive_all[band] for band in range(bands)
    ]
    table = basis_rows(bands)
    solve = np.linalg.solve(table.T @ table, table.T)
    fitted = None
    for i in range(4):
        value = float(solve[i, 0]) * sums[0]
        for band in range(1, bands):
            value = value + float(solve[i, band]) * sums[band]
        result[2 + i] = value
        fitted = value if i == 0 else fitted + basis[i] * value
    result[1] = base - step_all[my_band, 0:1] * drive - fitted


def spread(result, jones_out, duals_out, cons_out):
    rows = jones_out.shape[2]
    for part in range(2):
        lanes = slice(part * rows, (part + 1) * rows)
        cut = slice(4 * part, 4 * part + 4)
        jones_out[cut] = result[0, :, lanes].reshape(4, DIRS, rows)
        duals_out[cut] = result[1, :, lanes].reshape(4, DIRS, rows)
        for i in range(4):
            cons_out[i, cut] = result[2 + i, :, lanes].reshape(4, DIRS, rows)


def local(
    visibilities,
    flag_mask,
    stations,
    directions,
    intensity,
    polarized,
    spectral,
    clusters,
    jones_gains,
    scaled_duals,
    consensus,
):
    bands = lax.axis_size("freq")
    blocks = lax.axis_size("stn")
    rows, total = flag_mask.shape
    comps = clusters.shape[0]
    vmem = pl.BlockSpec(memory_space=pltpu.VMEM)
    block_sem = pltpu.SemaphoreType.DMA((blocks - 1,))
    band_sem = pltpu.SemaphoreType.DMA((bands - 1,))
    result = pl.pallas_call(
        functools.partial(kernel, bands, blocks),
        out_shape=jax.ShapeDtypeStruct((6, 4 * DIRS, 2 * rows), F32),
        in_specs=[vmem] * 11,
        out_specs=vmem,
        scratch_shapes=[
            pltpu.VMEM((blocks, 4 * DIRS, 2 * rows), F32),
            pltpu.VMEM((blocks, 8, 2 * rows), F32),
            pltpu.VMEM((blocks, 5, rows, 2 * rows), BF16),
            pltpu.VMEM((blocks, 5, rows, 2 * rows), BF16),
            pltpu.VMEM((bands, 4 * DIRS, 2 * rows), F32),
            pltpu.VMEM((bands, 4 * DIRS, 2 * rows), F32),
            pltpu.VMEM((blocks, 8, 2 * rows), F32),
            pltpu.VMEM((bands, 8, 2 * rows), F32),
            pltpu.VMEM((LANES, comps), BF16),
            pltpu.VMEM((32 * DIRS, comps), BF16),
            pltpu.VMEM((DIRS, 8, LANES), F32),
            pltpu.VMEM((DIRS, LANES, 8), F32),
            pltpu.VMEM((DIRS, rows, 8), F32),
            pltpu.VMEM((8, DIRS, total), F32),
            pltpu.VMEM((DIRS, 8, 8, total), F32),
            pltpu.VMEM((8, total), F32),
            pltpu.VMEM((3 * rows, 2 * LANES), BF16),
            pltpu.VMEM((3 * rows, 2 * LANES), BF16),
            pltpu.VMEM((2 * LANES, 2 * total), BF16),
            pltpu.VMEM((2 * LANES, 2 * total), BF16),
            pltpu.VMEM((DIRS, 3 * rows, 2 * total), F32),
            pltpu.VMEM((DIRS, 8, 8, total), F32),
            pltpu.VMEM((8, rows, total), F32),
            pltpu.VMEM((rows, total), F32),
            pltpu.VMEM((rows, 8 * DIRS), F32),
        ]
        + [block_sem] * 8
        + [band_sem] * 6,
        compiler_params=pltpu.CompilerParams(
            collective_id=0, has_side_effects=True, vmem_limit_bytes=58 * 1024 * 1024
        ),
    )(
        visibilities[0],
        flag_mask,
        stations,
        directions,
        intensity,
        polarized,
        spectral,
        clusters,
        jones_gains[0],
        scaled_duals[0],
        consensus,
    )
    outs = pl.pallas_call(
        spread,
        out_shape=(
            jax.ShapeDtypeStruct((8, DIRS, rows), F32),
            jax.ShapeDtypeStruct((8, DIRS, rows), F32),
            jax.ShapeDtypeStruct((4, 8, DIRS, rows), F32),
        ),
        in_specs=[vmem],
        out_specs=(vmem, vmem, vmem),
    )(result)
    return (outs[0][None], outs[1][None], outs[2])


def solution(mesh):
    placed = (
        P("freq", None, "stn", None),
        P("stn", None),
        P(None, "stn"),
        P(),
        P(),
        P(),
        P(),
        P(),
        P("freq", None, None, "stn"),
        P("freq", None, None, "stn"),
        P(None, None, None, "stn"),
    )
    return jax.shard_map(
        local,
        mesh=mesh,
        in_specs=placed,
        out_specs=(
            P("freq", None, None, "stn"),
            P("freq", None, None, "stn"),
            P(None, None, None, "stn"),
        ),
        check_vma=False,
    )
```

```python
import functools

import jax
import jax.numpy as jnp
import numpy as np
from jax import lax
from jax.experimental import pallas as pl
from jax.experimental.pallas import tpu as pltpu
from jax.sharding import PartitionSpec as P

DIRS = 16
LANES = 128
BF16_ROWS = 16
PENALTY = 40.0
STEP_SIZE = 0.5
MESH = pl.DeviceIdType.MESH
F32 = jnp.float32
BF16 = jnp.bfloat16


def turn_series(count):
    square = np.linspace(0.0, 0.25, 4001)
    root = np.sqrt(square)
    cosine = np.cos(2 * np.pi * root)
    sine = -2 * np.pi * np.sinc(2 * root)
    fits = []
    for target in (cosine, sine):
        fit = np.polynomial.chebyshev.Chebyshev.fit(square, target, count - 1, domain=[0.0, 0.25])
        fits.append([float(c) for c in fit.convert(kind=np.polynomial.Polynomial).coef])
    return fits


COS_SERIES, SIN_SERIES = turn_series(7)


def basis_rows(band_count):
    centre = (2.0 * np.arange(band_count) + 1.0) / band_count - 1.0
    return np.stack(
        [
            np.ones_like(centre),
            centre,
            0.5 * (3.0 * centre**2 - 1.0),
            0.5 * (5.0 * centre**3 - 3.0 * centre),
        ],
        axis=1,
    )


def horner(series, value):
    total = value * series[-1] + series[-2]
    for coefficient in series[-3::-1]:
        total = total * value + coefficient
    return total


def phasor(turns):
    part = turns - jnp.floor(turns + 0.5)
    square = part * part
    return horner(COS_SERIES, square).astype(BF16), (horner(SIN_SERIES, square) * part).astype(BF16)


def by_station(value):
    return value.reshape(8 * DIRS, value.shape[2]).T


def kernel(
    bands,
    blocks,
    vis_ref,
    mask_ref,
    stations_ref,
    dirs_ref,
    flux_ref,
    pol_ref,
    index_ref,
    clusters_ref,
    gains_ref,
    duals_ref,
    cons_ref,
    result,
    near_all,
    place_all,
    vis_send,
    vis_recv,
    base_all,
    drive_all,
    norm_all,
    oh_rank,
    sky_lhs,
    sky_rows,
    sky_cols,
    jones_cols,
    jones_rows,
    jones_far,
    place_rows,
    left_all,
    right_even,
    right_odd,
    coh,
    far_terms,
    wide,
    model,
    mask_sum,
    grad_cols,
    near_ssem,
    near_rsem,
    place_ssem,
    place_rsem,
    vis_ssem,
    vis_rsem,
    norm_ssem,
    norm_rsem,
    base_ssem,
    base_rsem,
    drive_ssem,
    drive_rsem,
):
    my_band = lax.axis_index("freq")
    my_block = lax.axis_index("stn")
    rows = gains_ref.shape[2]
    total = vis_ref.shape[2]
    comps = clusters_ref.shape[0]
    span = comps // DIRS

    barrier = pltpu.get_barrier_semaphore()
    stn_peers = [lax.rem(my_block + d, blocks) for d in range(1, blocks)]
    freq_peers = [lax.rem(my_band + d, bands) for d in range(1, bands)]
    slots = bands * blocks
    my_slot = my_band * blocks + my_block

    def slot_device(distance):
        slot = lax.rem(my_slot + distance, slots)
        return (slot // blocks, lax.rem(slot, blocks))

    @pl.loop(1, slots)
    def greet(distance):
        pl.semaphore_signal(
            barrier, inc=1, device_id=slot_device(distance), device_id_type=MESH
        )

    def send(source, target, ssem, rsem, at, device):
        copy = pltpu.make_async_remote_copy(
            src_ref=source,
            dst_ref=target,
            send_sem=ssem.at[at],
            recv_sem=rsem.at[at],
            device_id=device,
            device_id_type=MESH,
        )
        copy.start()
        return copy

    def to_blocks(source_of, target, ssem, rsem):
        return [
            send(source_of(peer), target.at[my_block], ssem, rsem, at, (my_band, peer))
            for at, peer in enumerate(stn_peers)
        ]

    def to_bands(target, ssem, rsem, first=0):
        return [
            send(target, target, ssem, rsem, first + at, (peer, my_block))
            for at, peer in enumerate(freq_peers)
        ]

    def norm_copy(distance):
        return pltpu.make_async_remote_copy(
            src_ref=norm_all.at[my_slot],
            dst_ref=norm_all.at[my_slot],
            send_sem=norm_ssem.at[distance],
            recv_sem=norm_rsem.at[distance],
            device_id=slot_device(distance),
            device_id_type=MESH,
        )

    gains = gains_ref[...]
    half = 4 * DIRS
    near_all[my_block] = jnp.concatenate(
        [gains[0:4].reshape(half, rows), gains[4:8].reshape(half, rows)], 1
    )
    own_jones = by_station(gains)
    place_all[my_block] = jnp.zeros((8, 2 * rows), F32)
    place_all[my_block, 0:3, 0:rows] = stations_ref[...]
    base_all[my_band] = own_jones + by_station(duals_ref[...])

    mask = mask_ref[...].astype(F32)
    for pair in range(5):
        if pair < 4:
            first, second = vis_ref[2 * pair] * mask, vis_ref[2 * pair + 1] * mask
        else:
            first = second = mask
        turned = jnp.concatenate([first, second], 0).T.astype(BF16)
        for block in range(blocks):
            vis_send[block, pair] = turned[block * rows : (block + 1) * rows]
        if pair < 4:
            wide[2 * pair] = first
            wide[2 * pair + 1] = second
        else:
            mask_sum[...] = first
    pl.semaphore_wait(barrier, slots - 1)
    place_copies = to_blocks(
        lambda peer: place_all.at[my_block], place_all, place_ssem, place_rsem
    )
    near_copies = to_blocks(lambda peer: near_all.at[my_block], near_all, near_ssem, near_rsem)
    vis_copies = to_blocks(lambda peer: vis_send.at[peer], vis_recv, vis_ssem, vis_rsem)
    base_copies = to_bands(base_all.at[my_band], base_ssem, base_rsem)
    vis_recv[my_block] = vis_send[my_block]

    clusters = clusters_ref[...].reshape(1, comps)
    member = (lax.broadcasted_iota(jnp.int32, (DIRS, comps), 0) == clusters).astype(F32)
    chunks = comps // LANES
    stacked = jnp.concatenate([member[:, c * LANES : (c + 1) * LANES] for c in range(chunks)], 0)
    before = (
        lax.broadcasted_iota(jnp.int32, (LANES, LANES), 0)
        < lax.broadcasted_iota(jnp.int32, (LANES, LANES), 1)
    ).astype(BF16)
    prefix = jnp.dot(stacked.astype(BF16), before, preferred_element_type=F32)
    running = jnp.zeros((DIRS, 1), F32)
    rank_iota = lax.broadcasted_iota(jnp.int32, (LANES, LANES), 0).astype(F32)
    for c in range(chunks):
        own = stacked[c * DIRS : (c + 1) * DIRS]
        rank = jnp.sum(own * (prefix[c * DIRS : (c + 1) * DIRS] + running), 0, keepdims=True)
        oh_rank[:, c * LANES : (c + 1) * LANES] = (rank_iota == rank).astype(BF16)
        running = running + jnp.sum(own, 1, keepdims=True)
    values = jnp.concatenate(
        [
            dirs_ref[...],
            flux_ref[...].reshape(1, comps),
            pol_ref[...],
            index_ref[...].reshape(1, comps),
            jnp.zeros((2, comps), F32),
        ],
        0,
    )
    high = values.astype(BF16).astype(F32)
    middle = (values - high).astype(BF16).astype(F32)
    low = values - high - middle
    parts = jnp.concatenate([high, middle, low, jnp.zeros_like(low)], 0)
    for k in range(DIRS):
        sky_lhs[32 * k : 32 * k + 32] = (member[k : k + 1] * parts).astype(BF16)
    sky = lax.dot_general(
        sky_lhs[...], oh_rank[...], (((1,), (1,)), ((), ())), preferred_element_type=F32
    ).reshape(DIRS, 4, 8, LANES)
    sky = (sky[:, 2] + sky[:, 1]) + sky[:, 0]
    sky_rows[...] = sky
    sky_turned = sky.reshape(DIRS * 8, LANES).T
    for k in range(DIRS):
        sky_cols[k] = sky_turned[:, 8 * k : 8 * k + 8]
        jones_cols[k] = gains[:, k, :].T
    zero_rows = jnp.zeros((LANES - span, 2 * total), BF16)
    for right in (right_even, right_odd):
        right[span:LANES] = zero_rows
        right[LANES + span :] = zero_rows
    band_number = my_band.astype(F32)
    ratio = 0.5 + 3.0 * (band_number + 0.5) / bands
    log_ratio = jnp.log(jnp.full((8, LANES), ratio, F32))[0:1]
    own_place = stations_ref[...].T

    def n_less(l_value, m_value):
        return jnp.sqrt(1.0 - l_value * l_value - m_value * m_value) - 1.0

    def geometry(l_value, m_value, n_value, places):
        return ratio * (l_value * places[0] + m_value * places[1] + n_value * places[2])

    @pl.loop(0, DIRS)
    def build_left(k):
        row = sky_rows[k]
        factor = jnp.exp(row[5:6] * log_ratio)
        weights = (
            (row[2:3] + row[3:4]) * factor,
            row[4:5] * factor,
            (row[2:3] - row[3:4]) * factor,
        )
        step = 2 * BF16_ROWS
        for low in range(0, rows, step):
            places = [own_place[low : low + step, a : a + 1] for a in range(3)]
            turns = geometry(row[0:1], row[1:2], n_less(row[0:1], row[1:2]), places)
            own_r, own_i = (value.astype(F32) for value in phasor(turns))
            for at, weight in enumerate(weights):
                cut = slice(at * rows + low, at * rows + low + step)
                left_all[k, cut, 0:LANES] = (own_r * weight).astype(BF16)
                left_all[k, cut, LANES:] = (own_i * weight).astype(BF16)

    for copy in place_copies:
        copy.wait()
    for block in range(blocks):
        place_rows[:, block * rows : (block + 1) * rows] = place_all[block, :, 0:rows]

    def build(k, right):
        step = 2 * BF16_ROWS
        places = [place_rows[a : a + 1, :] for a in range(3)]
        low = 0
        while low < span:
            high = min(low + step, span)
            l_col, m_col = sky_cols[k, low:high, 0:1], sky_cols[k, low:high, 1:2]
            n_col = n_less(l_col, m_col)
            for tile in range(0, total, LANES):
                lanes = slice(tile, tile + LANES)
                turns = geometry(l_col, m_col, n_col, [place[:, lanes] for place in places])
                far_r, far_i = phasor(turns)
                right[low:high, lanes] = far_r
                right[low:high, total + tile : total + tile + LANES] = -far_i
                right[LANES + low : LANES + high, lanes] = far_i
                right[LANES + low : LANES + high, total + tile : total + tile + LANES] = far_r
            low = high

    def multiply(k, right):
        coh[k] = jnp.dot(left_all[k], right[...], preferred_element_type=F32)

    build(0, right_even)

    @pl.loop(0, DIRS // 2 - 1)
    def coherencies(at):
        build(2 * at + 1, right_odd)
        multiply(2 * at, right_even)
        build(2 * at + 2, right_even)
        multiply(2 * at + 1, right_odd)

    build(DIRS - 1, right_odd)
    multiply(DIRS - 2, right_even)
    multiply(DIRS - 1, right_odd)

    for copy in near_copies:
        copy.wait()
    for block in range(blocks):
        cut = slice(block * rows, (block + 1) * rows)
        near = near_all[block]
        jones_rows[0:4, :, cut] = near[:, 0:rows].reshape(4, DIRS, rows)
        jones_rows[4:8, :, cut] = near[:, rows:].reshape(4, DIRS, rows)
    for k in range(DIRS):
        for at in range(8):
            jones_far[k, at] = jnp.broadcast_to(jones_rows[at, k : k + 1, :], (8, total))
    def finish_wide():
        for copy in vis_copies:
            copy.wait()
        for i in range(2):
            for j in range(2):
                for part in range(2):
                    lanes = slice(part * rows, (part + 1) * rows)
                    other = jnp.concatenate(
                        [vis_recv[block, 2 * j + i, :, lanes].astype(F32) for block in range(blocks)],
                        1,
                    )
                    at = 2 * (2 * i + j) + part
                    wide[at] = wide[at] + other if part == 0 else wide[at] - other
        mask_sum[...] += jnp.concatenate(
            [vis_recv[block, 4, :, 0:rows].astype(F32) for block in range(blocks)], 1
        )

    lane = lax.broadcasted_iota(jnp.int32, (8, 8 * DIRS), 1)

    kept = far_terms.shape[2]
    tiles = [slice(tile, tile + LANES) for tile in range(0, total, LANES)]

    def model_rows(row_at):
        cut = pl.ds(pl.multiple_of(row_at * 8, 8), 8)
        kept_cut = cut if kept == rows else slice(0, 8)

        def add_model(k, sums):
            near = jones_cols[k, cut, :]
            near = [jnp.broadcast_to(near[:, at : at + 1], (8, LANES)) for at in range(8)]
            done = []
            for tile, lanes in enumerate(tiles):
                far_lanes = slice(total + tile * LANES, total + (tile + 1) * LANES)
                entries = []
                for at in range(3):
                    rows_at = pl.ds(pl.multiple_of(at * rows + row_at * 8, 8), 8)
                    entries.append((coh[k, rows_at, lanes], coh[k, rows_at, far_lanes]))
                matrix = ((entries[0], entries[1]), (entries[1], entries[2]))
                own = list(sums[8 * tile : 8 * tile + 8])
                for el in range(2):
                    c_r, c_i, d_r, d_i = (jones_far[k, 4 * el + a, :, lanes] for a in range(4))
                    for m in range(2):
                        (a_r, a_i), (b_r, b_i) = matrix[m]
                        y_r = (a_r * c_r + a_i * c_i) + (b_r * d_r + b_i * d_i)
                        y_i = (a_i * c_r - a_r * c_i) + (b_i * d_r - b_r * d_i)
                        far_terms[k, 4 * m + 2 * el, kept_cut, lanes] = y_r
                        far_terms[k, 4 * m + 2 * el + 1, kept_cut, lanes] = y_i
                        for i in range(2):
                            p_r, p_i = near[4 * i + 2 * m], near[4 * i + 2 * m + 1]
                            at = 4 * i + 2 * el
                            own[at] = own[at] + (p_r * y_r - p_i * y_i)
                            own[at + 1] = own[at + 1] + (p_r * y_i + p_i * y_r)
                done += own
            return tuple(done)

        sums = lax.fori_loop(
            0,
            DIRS,
            add_model,
            tuple(jnp.zeros((8, LANES), F32) for _ in range(8 * len(tiles))),
            unroll=2,
        )
        for tile, lanes in enumerate(tiles):
            for at in range(8):
                model[at, cut, lanes] = sums[8 * tile + at]

    def gradient_rows(row_at):
        cut = pl.ds(pl.multiple_of(row_at * 8, 8), 8)
        kept_cut = cut if kept == rows else slice(0, 8)
        w = [
            [
                wide[at, cut, lanes] - mask_sum[cut, lanes] * model[at, cut, lanes]
                for at in range(8)
            ]
            for lanes in tiles
        ]

        def add_gradient(k, columns):
            totals = [None] * 8
            for tile, lanes in enumerate(tiles):
                y = [far_terms[k, at, kept_cut, lanes] for at in range(8)]
                for i in range(2):
                    for j in range(2):
                        at = 4 * i + 2 * j
                        for m in range(2):
                            w_r, w_i = w[tile][4 * i + 2 * m], w[tile][4 * i + 2 * m + 1]
                            y_r, y_i = y[4 * j + 2 * m], y[4 * j + 2 * m + 1]
                            both = (w_r * y_r + w_i * y_i, w_i * y_r - w_r * y_i)
                            for part in range(2):
                                old = totals[at + part]
                                totals[at + part] = both[part] if old is None else old + both[part]
            for at in range(8):
                summed = jnp.sum(totals[at], 1, keepdims=True)
                columns = jnp.where(lane == at * DIRS + k, summed, columns)
            return columns

        grad_cols[cut] = lax.fori_loop(
            0, DIRS, add_gradient, jnp.zeros((8, 8 * DIRS), F32), unroll=4
        )

    centre = (2.0 * band_number + 1.0) / bands - 1.0
    basis = (
        1.0,
        centre,
        0.5 * (3.0 * centre * centre - 1.0),
        0.5 * (5.0 * centre * centre * centre - 3.0 * centre),
    )
    if kept == rows:
        pl.loop(0, rows // 8)(model_rows)
    poly = cons_ref[0]
    for i in range(1, 4):
        poly = poly + basis[i] * cons_ref[i]
    pull = PENALTY / 2.0 * (base_all[my_band] - by_station(poly))
    finish_wide()

    drive_copies = []
    squares = jnp.zeros((8, 8 * DIRS), F32)
    for part in range(2):

        @pl.loop(part * rows // 16, (part + 1) * rows // 16)
        def gradient(row_at):
            if kept != rows:
                model_rows(row_at)
            gradient_rows(row_at)

        cut = slice(part * rows // 2, (part + 1) * rows // 2)
        piece = pull[cut] - grad_cols[cut]
        drive_all[my_band, cut] = piece
        squares = squares + jnp.sum((piece * piece).reshape(-1, 8, 8 * DIRS), 0)
        if part == 1:
            norm_all[my_slot] = jnp.sum(squares, 0, keepdims=True)

            @pl.loop(1, slots)
            def send_norms(distance):
                norm_copy(distance).start()

        drive_copies += to_bands(
            drive_all.at[my_band, cut], drive_ssem, drive_rsem, part * (bands - 1)
        )

    @pl.loop(1, slots)
    def wait_norms(distance):
        norm_copy(distance).wait()

    squares = jnp.concatenate(
        [jnp.sum(norm_all[band * blocks : (band + 1) * blocks], 0) for band in range(bands)], 0
    )
    mean = jnp.sum(squares, 1, keepdims=True) / (8 * DIRS * total)
    steps = STEP_SIZE / jnp.sqrt(mean + 1e-06)
    for copy in base_copies + drive_copies:
        copy.wait()
    sums = [
        base_all[band] - steps[band : band + 1] * drive_all[band] for band in range(bands)
    ]
    table = basis_rows(bands)
    solve = np.linalg.solve(table.T @ table, table.T)
    fitted = None
    for i in range(4):
        value = float(solve[i, 0]) * sums[0]
        for band in range(1, bands):
            value = value + float(solve[i, band]) * sums[band]
        result[2 + i] = value
        fitted = value if i == 0 else fitted + basis[i] * value
    squares = jnp.sum(norm_all[pl.ds(my_band * blocks, blocks)], 0)
    mean = jnp.sum(squares, 1, keepdims=True) / (8 * DIRS * total)
    jones_next = own_jones - STEP_SIZE / jnp.sqrt(mean + 1e-06) * drive_all[my_band]
    result[0] = jones_next
    result[1] = by_station(duals_ref[...]) + jones_next - fitted


def spread(result, jones_out, duals_out, cons_out):
    shape = jones_out.shape
    jones_out[...] = result[0].T.reshape(shape)
    duals_out[...] = result[1].T.reshape(shape)
    for i in range(4):
        cons_out[i] = result[2 + i].T.reshape(shape)


def local(
    visibilities,
    flag_mask,
    stations,
    directions,
    intensity,
    polarized,
    spectral,
    clusters,
    jones_gains,
    scaled_duals,
    consensus,
):
    bands = lax.axis_size("freq")
    blocks = lax.axis_size("stn")
    rows, total = flag_mask.shape
    comps = clusters.shape[0]
    kept = rows if DIRS * 8 * rows * total * 4 <= 2**24 else 8
    vmem = pl.BlockSpec(memory_space=pltpu.VMEM)
    block_sem = pltpu.SemaphoreType.DMA((blocks - 1,))
    band_sem = pltpu.SemaphoreType.DMA((bands - 1,))
    result = pl.pallas_call(
        functools.partial(kernel, bands, blocks),
        out_shape=jax.ShapeDtypeStruct((6, rows, 8 * DIRS), F32),
        in_specs=[vmem] * 11,
        out_specs=vmem,
        scratch_shapes=[
            pltpu.VMEM((blocks, 4 * DIRS, 2 * rows), F32),
            pltpu.VMEM((blocks, 8, 2 * rows), F32),
            pltpu.VMEM((blocks, 5, rows, 2 * rows), BF16),
            pltpu.VMEM((blocks, 5, rows, 2 * rows), BF16),
            pltpu.VMEM((bands, rows, 8 * DIRS), F32),
            pltpu.VMEM((bands, rows, 8 * DIRS), F32),
            pltpu.VMEM((bands * blocks, 1, 8 * DIRS), F32),
            pltpu.VMEM((LANES, comps), BF16),
            pltpu.VMEM((32 * DIRS, comps), BF16),
            pltpu.VMEM((DIRS, 8, LANES), F32),
            pltpu.VMEM((DIRS, LANES, 8), F32),
            pltpu.VMEM((DIRS, rows, 8), F32),
            pltpu.VMEM((8, DIRS, total), F32),
            pltpu.VMEM((DIRS, 8, 8, total), F32),
            pltpu.VMEM((8, total), F32),
            pltpu.VMEM((DIRS, 3 * rows, 2 * LANES), BF16),
            pltpu.VMEM((2 * LANES, 2 * total), BF16),
            pltpu.VMEM((2 * LANES, 2 * total), BF16),
            pltpu.VMEM((DIRS, 3 * rows, 2 * total), F32),
            pltpu.VMEM((DIRS, 8, kept, total), F32),
            pltpu.VMEM((8, rows, total), F32),
            pltpu.VMEM((8, rows, total), F32),
            pltpu.VMEM((rows, total), F32),
            pltpu.VMEM((rows, 8 * DIRS), F32),
        ]
        + [block_sem] * 6
        + [pltpu.SemaphoreType.DMA((bands * blocks,))] * 2
        + [band_sem] * 2
        + [pltpu.SemaphoreType.DMA((2 * (bands - 1),))] * 2,
        compiler_params=pltpu.CompilerParams(
            collective_id=0, has_side_effects=True, vmem_limit_bytes=58 * 1024 * 1024
        ),
    )(
        visibilities[0],
        flag_mask,
        stations,
        directions,
        intensity,
        polarized,
        spectral,
        clusters,
        jones_gains[0],
        scaled_duals[0],
        consensus,
    )
    outs = pl.pallas_call(
        spread,
        out_shape=(
            jax.ShapeDtypeStruct((8, DIRS, rows), F32),
            jax.ShapeDtypeStruct((8, DIRS, rows), F32),
            jax.ShapeDtypeStruct((4, 8, DIRS, rows), F32),
        ),
        in_specs=[vmem],
        out_specs=(vmem, vmem, vmem),
    )(result)
    return (outs[0][None], outs[1][None], outs[2])


def solution(mesh):
    placed = (
        P("freq", None, "stn", None),
        P("stn", None),
        P(None, "stn"),
        P(),
        P(),
        P(),
        P(),
        P(),
        P("freq", None, None, "stn"),
        P("freq", None, None, "stn"),
        P(None, None, None, "stn"),
    )
    return jax.shard_map(
        local,
        mesh=mesh,
        in_specs=placed,
        out_specs=(
            P("freq", None, None, "stn"),
            P("freq", None, None, "stn"),
            P(None, None, None, "stn"),
        ),
        check_vma=False,
    )
```

```python
import functools

import jax
import jax.numpy as jnp
import numpy as np
from jax import lax
from jax.experimental import pallas as pl
from jax.experimental.pallas import tpu as pltpu
from jax.sharding import PartitionSpec as P

DIRS = 16
LANES = 128
BF16_ROWS = 16
PENALTY = 40.0
STEP_SIZE = 0.5
MESH = pl.DeviceIdType.MESH
F32 = jnp.float32
BF16 = jnp.bfloat16


def turn_series(count):
    square = np.linspace(0.0, 0.25, 4001)
    root = np.sqrt(square)
    cosine = np.cos(2 * np.pi * root)
    sine = -2 * np.pi * np.sinc(2 * root)
    fits = []
    for target in (cosine, sine):
        fit = np.polynomial.chebyshev.Chebyshev.fit(square, target, count - 1, domain=[0.0, 0.25])
        fits.append([float(c) for c in fit.convert(kind=np.polynomial.Polynomial).coef])
    return fits


COS_SERIES, SIN_SERIES = turn_series(6)


def basis_rows(band_count):
    centre = (2.0 * np.arange(band_count) + 1.0) / band_count - 1.0
    return np.stack(
        [
            np.ones_like(centre),
            centre,
            0.5 * (3.0 * centre**2 - 1.0),
            0.5 * (5.0 * centre**3 - 3.0 * centre),
        ],
        axis=1,
    )


def horner(series, value):
    total = value * series[-1] + series[-2]
    for coefficient in series[-3::-1]:
        total = total * value + coefficient
    return total


def phasor(turns):
    part = turns - jnp.floor(turns + 0.5)
    square = part * part
    return horner(COS_SERIES, square).astype(BF16), (horner(SIN_SERIES, square) * part).astype(BF16)


def by_station(value):
    return value.reshape(8 * DIRS, value.shape[2]).T


def kernel(
    bands,
    blocks,
    vis_ref,
    mask_ref,
    stations_ref,
    dirs_ref,
    flux_ref,
    pol_ref,
    index_ref,
    clusters_ref,
    gains_ref,
    duals_ref,
    cons_ref,
    result,
    near_all,
    place_all,
    vis_send,
    vis_recv,
    base_all,
    drive_all,
    norm_all,
    oh_rank,
    sky_lhs,
    sky_rows,
    sky_cols,
    jones_cols,
    jones_near,
    jones_rows,
    jones_far,
    place_rows,
    left_all,
    right_even,
    right_odd,
    coh,
    far_terms,
    wide,
    model,
    mask_sum,
    grad_cols,
    near_ssem,
    near_rsem,
    place_ssem,
    place_rsem,
    vis_ssem,
    vis_rsem,
    norm_ssem,
    norm_rsem,
    base_ssem,
    base_rsem,
    drive_ssem,
    drive_rsem,
):
    my_band = lax.axis_index("freq")
    my_block = lax.axis_index("stn")
    rows = gains_ref.shape[2]
    total = vis_ref.shape[2]
    comps = clusters_ref.shape[0]
    span = comps // DIRS

    barrier = pltpu.get_barrier_semaphore()
    stn_peers = [lax.rem(my_block + d, blocks) for d in range(1, blocks)]
    freq_peers = [lax.rem(my_band + d, bands) for d in range(1, bands)]
    slots = bands * blocks
    my_slot = my_band * blocks + my_block

    def slot_device(distance):
        slot = lax.rem(my_slot + distance, slots)
        return (slot // blocks, lax.rem(slot, blocks))

    @pl.loop(1, slots)
    def greet(distance):
        pl.semaphore_signal(
            barrier, inc=1, device_id=slot_device(distance), device_id_type=MESH
        )

    def send(source, target, ssem, rsem, at, device):
        copy = pltpu.make_async_remote_copy(
            src_ref=source,
            dst_ref=target,
            send_sem=ssem.at[at],
            recv_sem=rsem.at[at],
            device_id=device,
            device_id_type=MESH,
        )
        copy.start()
        return copy

    def to_blocks(source_of, target, ssem, rsem):
        return [
            send(source_of(peer), target.at[my_block], ssem, rsem, at, (my_band, peer))
            for at, peer in enumerate(stn_peers)
        ]

    def to_bands(target, ssem, rsem, first=0):
        return [
            send(target, target, ssem, rsem, first + at, (peer, my_block))
            for at, peer in enumerate(freq_peers)
        ]

    def norm_copy(distance):
        return pltpu.make_async_remote_copy(
            src_ref=norm_all.at[my_slot],
            dst_ref=norm_all.at[my_slot],
            send_sem=norm_ssem.at[distance],
            recv_sem=norm_rsem.at[distance],
            device_id=slot_device(distance),
            device_id_type=MESH,
        )

    gains = gains_ref[...]
    half = 4 * DIRS
    near_all[my_block] = jnp.concatenate(
        [gains[0:4].reshape(half, rows), gains[4:8].reshape(half, rows)], 1
    )
    own_jones = by_station(gains)
    place_all[my_block] = jnp.zeros((8, 2 * rows), F32)
    place_all[my_block, 0:3, 0:rows] = stations_ref[...]
    base_all[my_band] = own_jones + by_station(duals_ref[...])

    mask = mask_ref[...].astype(F32)
    for pair in range(5):
        if pair < 4:
            first, second = vis_ref[2 * pair] * mask, vis_ref[2 * pair + 1] * mask
        else:
            first = second = mask
        turned = jnp.concatenate([first, second], 0).T.astype(BF16)
        for block in range(blocks):
            vis_send[block, pair] = turned[block * rows : (block + 1) * rows]
        if pair < 4:
            wide[2 * pair] = first
            wide[2 * pair + 1] = second
        else:
            mask_sum[...] = first
    pl.semaphore_wait(barrier, slots - 1)
    place_copies = to_blocks(
        lambda peer: place_all.at[my_block], place_all, place_ssem, place_rsem
    )
    near_copies = to_blocks(lambda peer: near_all.at[my_block], near_all, near_ssem, near_rsem)
    vis_copies = to_blocks(lambda peer: vis_send.at[peer], vis_recv, vis_ssem, vis_rsem)
    base_copies = to_bands(base_all.at[my_band], base_ssem, base_rsem)
    vis_recv[my_block] = vis_send[my_block]

    clusters = clusters_ref[...].reshape(1, comps)
    member = (lax.broadcasted_iota(jnp.int32, (DIRS, comps), 0) == clusters).astype(F32)
    chunks = comps // LANES
    stacked = jnp.concatenate([member[:, c * LANES : (c + 1) * LANES] for c in range(chunks)], 0)
    before = (
        lax.broadcasted_iota(jnp.int32, (LANES, LANES), 0)
        < lax.broadcasted_iota(jnp.int32, (LANES, LANES), 1)
    ).astype(BF16)
    prefix = jnp.dot(stacked.astype(BF16), before, preferred_element_type=F32)
    running = jnp.zeros((DIRS, 1), F32)
    rank_iota = lax.broadcasted_iota(jnp.int32, (LANES, LANES), 0).astype(F32)
    for c in range(chunks):
        own = stacked[c * DIRS : (c + 1) * DIRS]
        rank = jnp.sum(own * (prefix[c * DIRS : (c + 1) * DIRS] + running), 0, keepdims=True)
        oh_rank[:, c * LANES : (c + 1) * LANES] = (rank_iota == rank).astype(BF16)
        running = running + jnp.sum(own, 1, keepdims=True)
    values = jnp.concatenate(
        [
            dirs_ref[...],
            flux_ref[...].reshape(1, comps),
            pol_ref[...],
            index_ref[...].reshape(1, comps),
            jnp.zeros((2, comps), F32),
        ],
        0,
    )
    high = values.astype(BF16).astype(F32)
    middle = (values - high).astype(BF16).astype(F32)
    low = values - high - middle
    parts = jnp.concatenate([high, middle, low, jnp.zeros_like(low)], 0)
    for k in range(DIRS):
        sky_lhs[32 * k : 32 * k + 32] = (member[k : k + 1] * parts).astype(BF16)
    sky = lax.dot_general(
        sky_lhs[...], oh_rank[...], (((1,), (1,)), ((), ())), preferred_element_type=F32
    ).reshape(DIRS, 4, 8, LANES)
    sky = (sky[:, 2] + sky[:, 1]) + sky[:, 0]
    band_number = my_band.astype(F32)
    ratio = 0.5 + 3.0 * (band_number + 0.5) / bands
    l_all, m_all, i_all, q_all, u_all, slope = (sky[:, at] for at in range(6))
    factor = jnp.exp(slope * jnp.log(jnp.full((DIRS, LANES), ratio, F32)))
    n_all = jnp.sqrt(1.0 - l_all * l_all - m_all * m_all) - 1.0
    sky_rows[:, 0] = l_all
    sky_rows[:, 1] = m_all
    sky_rows[:, 2] = n_all
    sky_rows[:, 3] = (i_all + q_all) * factor
    sky_rows[:, 4] = u_all * factor
    sky_rows[:, 5] = (i_all - q_all) * factor
    sky_rows[:, 6] = n_all
    sky_rows[:, 7] = n_all
    sky_turned = sky_rows[...].reshape(DIRS * 8, LANES).T
    for k in range(DIRS):
        sky_cols[k] = sky_turned[:, 8 * k : 8 * k + 8]
        jones_cols[k] = gains[:, k, :].T
    zero_rows = jnp.zeros((LANES - span, 2 * total), BF16)
    for right in (right_even, right_odd):
        right[span:LANES] = zero_rows
        right[LANES + span :] = zero_rows
    own_place = stations_ref[...].T * ratio

    def geometry(l_value, m_value, n_value, places):
        return l_value * places[0] + m_value * places[1] + n_value * places[2]

    @pl.loop(0, DIRS)
    def build_left(k):
        row = sky_rows[k]
        near = jones_cols[k]
        for at in range(8):
            jones_near[k, at] = jnp.broadcast_to(near[:, at : at + 1], (rows, LANES))
        step = 2 * BF16_ROWS
        for low in range(0, rows, step):
            places = [own_place[low : low + step, a : a + 1] for a in range(3)]
            turns = geometry(row[0:1], row[1:2], row[2:3], places)
            own_r, own_i = (value.astype(F32) for value in phasor(turns))
            for at in range(3):
                weight = row[3 + at : 4 + at]
                cut = slice(at * rows + low, at * rows + low + step)
                left_all[k, cut, 0:LANES] = (own_r * weight).astype(BF16)
                left_all[k, cut, LANES:] = (own_i * weight).astype(BF16)

    for copy in place_copies:
        copy.wait()
    for block in range(blocks):
        place_rows[:, block * rows : (block + 1) * rows] = place_all[block, :, 0:rows] * ratio

    def build(k, right):
        step = 2 * BF16_ROWS
        places = [place_rows[a : a + 1, :] for a in range(3)]
        low = 0
        while low < span:
            high = min(low + step, span)
            l_col, m_col, n_col = (sky_cols[k, low:high, at : at + 1] for at in range(3))
            for tile in range(0, total, LANES):
                lanes = slice(tile, tile + LANES)
                turns = geometry(l_col, m_col, n_col, [place[:, lanes] for place in places])
                far_r, far_i = phasor(turns)
                right[low:high, lanes] = far_r
                right[low:high, total + tile : total + tile + LANES] = -far_i
                right[LANES + low : LANES + high, lanes] = far_i
                right[LANES + low : LANES + high, total + tile : total + tile + LANES] = far_r
            low = high

    def multiply(k, right):
        coh[k] = jnp.dot(left_all[k], right[...], preferred_element_type=F32)

    build(0, right_even)

    @pl.loop(0, DIRS // 2 - 1)
    def coherencies(at):
        build(2 * at + 1, right_odd)
        multiply(2 * at, right_even)
        build(2 * at + 2, right_even)
        multiply(2 * at + 1, right_odd)

    build(DIRS - 1, right_odd)
    multiply(DIRS - 2, right_even)
    multiply(DIRS - 1, right_odd)

    for copy in near_copies:
        copy.wait()
    for block in range(blocks):
        cut = slice(block * rows, (block + 1) * rows)
        near = near_all[block]
        jones_rows[0:4, :, cut] = near[:, 0:rows].reshape(4, DIRS, rows)
        jones_rows[4:8, :, cut] = near[:, rows:].reshape(4, DIRS, rows)
    for k in range(DIRS):
        for at in range(8):
            jones_far[k, at] = jnp.broadcast_to(jones_rows[at, k : k + 1, :], (8, total))
    def finish_wide():
        for copy in vis_copies:
            copy.wait()
        for i in range(2):
            for j in range(2):
                for part in range(2):
                    lanes = slice(part * rows, (part + 1) * rows)
                    other = jnp.concatenate(
                        [vis_recv[block, 2 * j + i, :, lanes].astype(F32) for block in range(blocks)],
                        1,
                    )
                    at = 2 * (2 * i + j) + part
                    wide[at] = wide[at] + other if part == 0 else wide[at] - other
        mask_sum[...] += jnp.concatenate(
            [vis_recv[block, 4, :, 0:rows].astype(F32) for block in range(blocks)], 1
        )

    lane = lax.broadcasted_iota(jnp.int32, (8, 8 * DIRS), 1)

    kept = far_terms.shape[2]
    tiles = [slice(tile, tile + LANES) for tile in range(0, total, LANES)]

    def model_rows(row_at):
        cut = pl.ds(pl.multiple_of(row_at * 8, 8), 8)
        kept_cut = cut if kept == rows else slice(0, 8)

        def add_model(k, sums):
            near = [jones_near[k, at, cut] for at in range(8)]
            done = []
            for tile, lanes in enumerate(tiles):
                far_lanes = slice(total + tile * LANES, total + (tile + 1) * LANES)
                entries = []
                for at in range(3):
                    rows_at = pl.ds(pl.multiple_of(at * rows + row_at * 8, 8), 8)
                    entries.append((coh[k, rows_at, lanes], coh[k, rows_at, far_lanes]))
                matrix = ((entries[0], entries[1]), (entries[1], entries[2]))
                own = list(sums[8 * tile : 8 * tile + 8])
                for el in range(2):
                    c_r, c_i, d_r, d_i = (jones_far[k, 4 * el + a, :, lanes] for a in range(4))
                    for m in range(2):
                        (a_r, a_i), (b_r, b_i) = matrix[m]
                        y_r = (a_r * c_r + a_i * c_i) + (b_r * d_r + b_i * d_i)
                        y_i = (a_i * c_r - a_r * c_i) + (b_i * d_r - b_r * d_i)
                        far_terms[k, 4 * m + 2 * el, kept_cut, lanes] = y_r
                        far_terms[k, 4 * m + 2 * el + 1, kept_cut, lanes] = y_i
                        for i in range(2):
                            p_r, p_i = near[4 * i + 2 * m], near[4 * i + 2 * m + 1]
                            at = 4 * i + 2 * el
                            own[at] = own[at] + (p_r * y_r - p_i * y_i)
                            own[at + 1] = own[at + 1] + (p_r * y_i + p_i * y_r)
                done += own
            return tuple(done)

        sums = lax.fori_loop(
            0,
            DIRS,
            add_model,
            tuple(jnp.zeros((8, LANES), F32) for _ in range(8 * len(tiles))),
            unroll=4,
        )
        for tile, lanes in enumerate(tiles):
            for at in range(8):
                model[at, cut, lanes] = sums[8 * tile + at]

    def gradient_rows(row_at):
        cut = pl.ds(pl.multiple_of(row_at * 8, 8), 8)
        kept_cut = cut if kept == rows else slice(0, 8)
        w = [
            [
                wide[at, cut, lanes] - mask_sum[cut, lanes] * model[at, cut, lanes]
                for at in range(8)
            ]
            for lanes in tiles
        ]

        def add_gradient(k, columns):
            totals = [None] * 8
            for tile, lanes in enumerate(tiles):
                y = [far_terms[k, at, kept_cut, lanes] for at in range(8)]
                for i in range(2):
                    for j in range(2):
                        at = 4 * i + 2 * j
                        for m in range(2):
                            w_r, w_i = w[tile][4 * i + 2 * m], w[tile][4 * i + 2 * m + 1]
                            y_r, y_i = y[4 * j + 2 * m], y[4 * j + 2 * m + 1]
                            both = (w_r * y_r + w_i * y_i, w_i * y_r - w_r * y_i)
                            for part in range(2):
                                old = totals[at + part]
                                totals[at + part] = both[part] if old is None else old + both[part]
            for at in range(8):
                summed = jnp.sum(totals[at], 1, keepdims=True)
                columns = jnp.where(lane == at * DIRS + k, summed, columns)
            return columns

        grad_cols[cut] = lax.fori_loop(
            0, DIRS, add_gradient, jnp.zeros((8, 8 * DIRS), F32), unroll=8
        )

    centre = (2.0 * band_number + 1.0) / bands - 1.0
    basis = (
        1.0,
        centre,
        0.5 * (3.0 * centre * centre - 1.0),
        0.5 * (5.0 * centre * centre * centre - 3.0 * centre),
    )
    if kept == rows:
        pl.loop(0, rows // 8)(model_rows)
    poly = cons_ref[0]
    for i in range(1, 4):
        poly = poly + basis[i] * cons_ref[i]
    pull = PENALTY / 2.0 * (base_all[my_band] - by_station(poly))
    finish_wide()

    drive_copies = []
    squares = jnp.zeros((8, 8 * DIRS), F32)
    for part in range(2):

        @pl.loop(part * rows // 16, (part + 1) * rows // 16)
        def gradient(row_at):
            if kept != rows:
                model_rows(row_at)
            gradient_rows(row_at)

        cut = slice(part * rows // 2, (part + 1) * rows // 2)
        piece = pull[cut] - grad_cols[cut]
        drive_all[my_band, cut] = piece
        squares = squares + jnp.sum((piece * piece).reshape(-1, 8, 8 * DIRS), 0)
        if part == 1:
            norm_all[my_slot] = jnp.sum(squares, 0, keepdims=True)

            @pl.loop(1, slots)
            def send_norms(distance):
                norm_copy(distance).start()

        drive_copies += to_bands(
            drive_all.at[my_band, cut], drive_ssem, drive_rsem, part * (bands - 1)
        )

    @pl.loop(1, slots)
    def wait_norms(distance):
        norm_copy(distance).wait()

    squares = jnp.concatenate(
        [jnp.sum(norm_all[band * blocks : (band + 1) * blocks], 0) for band in range(bands)], 0
    )
    mean = jnp.sum(squares, 1, keepdims=True) / (8 * DIRS * total)
    steps = STEP_SIZE / jnp.sqrt(mean + 1e-06)
    for copy in base_copies + drive_copies:
        copy.wait()
    sums = [
        base_all[band] - steps[band : band + 1] * drive_all[band] for band in range(bands)
    ]
    table = basis_rows(bands)
    solve = np.linalg.solve(table.T @ table, table.T)
    fitted = None
    for i in range(4):
        value = float(solve[i, 0]) * sums[0]
        for band in range(1, bands):
            value = value + float(solve[i, band]) * sums[band]
        result[2 + i] = value
        fitted = value if i == 0 else fitted + basis[i] * value
    squares = jnp.sum(norm_all[pl.ds(my_band * blocks, blocks)], 0)
    mean = jnp.sum(squares, 1, keepdims=True) / (8 * DIRS * total)
    jones_next = own_jones - STEP_SIZE / jnp.sqrt(mean + 1e-06) * drive_all[my_band]
    result[0] = jones_next
    result[1] = by_station(duals_ref[...]) + jones_next - fitted


def spread(result, jones_out, duals_out, cons_out):
    shape = jones_out.shape
    jones_out[...] = result[0].T.reshape(shape)
    duals_out[...] = result[1].T.reshape(shape)
    for i in range(4):
        cons_out[i] = result[2 + i].T.reshape(shape)


def local(
    visibilities,
    flag_mask,
    stations,
    directions,
    intensity,
    polarized,
    spectral,
    clusters,
    jones_gains,
    scaled_duals,
    consensus,
):
    bands = lax.axis_size("freq")
    blocks = lax.axis_size("stn")
    rows, total = flag_mask.shape
    comps = clusters.shape[0]
    kept = rows if DIRS * 8 * rows * total * 4 <= 2**24 else 8
    vmem = pl.BlockSpec(memory_space=pltpu.VMEM)
    block_sem = pltpu.SemaphoreType.DMA((blocks - 1,))
    band_sem = pltpu.SemaphoreType.DMA((bands - 1,))
    result = pl.pallas_call(
        functools.partial(kernel, bands, blocks),
        out_shape=jax.ShapeDtypeStruct((6, rows, 8 * DIRS), F32),
        in_specs=[vmem] * 11,
        out_specs=vmem,
        scratch_shapes=[
            pltpu.VMEM((blocks, 4 * DIRS, 2 * rows), F32),
            pltpu.VMEM((blocks, 8, 2 * rows), F32),
            pltpu.VMEM((blocks, 5, rows, 2 * rows), BF16),
            pltpu.VMEM((blocks, 5, rows, 2 * rows), BF16),
            pltpu.VMEM((bands, rows, 8 * DIRS), F32),
            pltpu.VMEM((bands, rows, 8 * DIRS), F32),
            pltpu.VMEM((bands * blocks, 1, 8 * DIRS), F32),
            pltpu.VMEM((LANES, comps), BF16),
            pltpu.VMEM((32 * DIRS, comps), BF16),
            pltpu.VMEM((DIRS, 8, LANES), F32),
            pltpu.VMEM((DIRS, LANES, 8), F32),
            pltpu.VMEM((DIRS, rows, 8), F32),
            pltpu.VMEM((DIRS, 8, rows, LANES), F32),
            pltpu.VMEM((8, DIRS, total), F32),
            pltpu.VMEM((DIRS, 8, 8, total), F32),
            pltpu.VMEM((8, total), F32),
            pltpu.VMEM((DIRS, 3 * rows, 2 * LANES), BF16),
            pltpu.VMEM((2 * LANES, 2 * total), BF16),
            pltpu.VMEM((2 * LANES, 2 * total), BF16),
            pltpu.VMEM((DIRS, 3 * rows, 2 * total), F32),
            pltpu.VMEM((DIRS, 8, kept, total), F32),
            pltpu.VMEM((8, rows, total), F32),
            pltpu.VMEM((8, rows, total), F32),
            pltpu.VMEM((rows, total), F32),
            pltpu.VMEM((rows, 8 * DIRS), F32),
        ]
        + [block_sem] * 6
        + [pltpu.SemaphoreType.DMA((bands * blocks,))] * 2
        + [band_sem] * 2
        + [pltpu.SemaphoreType.DMA((2 * (bands - 1),))] * 2,
        compiler_params=pltpu.CompilerParams(
            collective_id=0, has_side_effects=True, vmem_limit_bytes=58 * 1024 * 1024
        ),
    )(
        visibilities[0],
        flag_mask,
        stations,
        directions,
        intensity,
        polarized,
        spectral,
        clusters,
        jones_gains[0],
        scaled_duals[0],
        consensus,
    )
    outs = pl.pallas_call(
        spread,
        out_shape=(
            jax.ShapeDtypeStruct((8, DIRS, rows), F32),
            jax.ShapeDtypeStruct((8, DIRS, rows), F32),
            jax.ShapeDtypeStruct((4, 8, DIRS, rows), F32),
        ),
        in_specs=[vmem],
        out_specs=(vmem, vmem, vmem),
    )(result)
    return (outs[0][None], outs[1][None], outs[2])


def solution(mesh):
    placed = (
        P("freq", None, "stn", None),
        P("stn", None),
        P(None, "stn"),
        P(),
        P(),
        P(),
        P(),
        P(),
        P("freq", None, None, "stn"),
        P("freq", None, None, "stn"),
        P(None, None, None, "stn"),
    )
    return jax.shard_map(
        local,
        mesh=mesh,
        in_specs=placed,
        out_specs=(
            P("freq", None, None, "stn"),
            P("freq", None, None, "stn"),
            P(None, None, None, "stn"),
        ),
        check_vma=False,
    )
```

```python
import functools

import jax
import jax.numpy as jnp
import numpy as np
from jax import lax
from jax.experimental import pallas as pl
from jax.experimental.pallas import tpu as pltpu
from jax.sharding import PartitionSpec as P

DIRS = 16
LANES = 128
BF16_ROWS = 16
PENALTY = 40.0
STEP_SIZE = 0.5
MESH = pl.DeviceIdType.MESH
F32 = jnp.float32
BF16 = jnp.bfloat16


def turn_series(count):
    square = np.linspace(0.0, 0.25, 4001)
    root = np.sqrt(square)
    cosine = np.cos(2 * np.pi * root)
    sine = -2 * np.pi * np.sinc(2 * root)
    fits = []
    for target in (cosine, sine):
        fit = np.polynomial.chebyshev.Chebyshev.fit(square, target, count - 1, domain=[0.0, 0.25])
        fits.append([float(c) for c in fit.convert(kind=np.polynomial.Polynomial).coef])
    return fits


COS_SERIES, SIN_SERIES = turn_series(6)


def basis_rows(band_count):
    centre = (2.0 * np.arange(band_count) + 1.0) / band_count - 1.0
    return np.stack(
        [
            np.ones_like(centre),
            centre,
            0.5 * (3.0 * centre**2 - 1.0),
            0.5 * (5.0 * centre**3 - 3.0 * centre),
        ],
        axis=1,
    )


def horner(series, value):
    total = value * series[-1] + series[-2]
    for coefficient in series[-3::-1]:
        total = total * value + coefficient
    return total


def phasor(turns):
    part = turns - jnp.floor(turns + 0.5)
    square = part * part
    return horner(COS_SERIES, square).astype(BF16), (horner(SIN_SERIES, square) * part).astype(BF16)


def by_station(value):
    return value.reshape(8 * DIRS, value.shape[2]).T


def kernel(
    bands,
    blocks,
    vis_ref,
    mask_ref,
    stations_ref,
    dirs_ref,
    flux_ref,
    pol_ref,
    index_ref,
    clusters_ref,
    gains_ref,
    duals_ref,
    cons_ref,
    result,
    near_all,
    place_all,
    vis_send,
    vis_recv,
    base_all,
    drive_all,
    norm_all,
    oh_rank,
    sky_lhs,
    sky_rows,
    sky_cols,
    jones_cols,
    jones_near,
    jones_rows,
    jones_far,
    place_rows,
    left_all,
    right_even,
    right_odd,
    coh,
    far_terms,
    wide,
    model,
    mask_sum,
    grad_cols,
    near_ssem,
    near_rsem,
    place_ssem,
    place_rsem,
    vis_ssem,
    vis_rsem,
    norm_ssem,
    norm_rsem,
    base_ssem,
    base_rsem,
    drive_ssem,
    drive_rsem,
):
    my_band = lax.axis_index("freq")
    my_block = lax.axis_index("stn")
    rows = gains_ref.shape[2]
    total = vis_ref.shape[2]
    comps = clusters_ref.shape[0]
    span = comps // DIRS

    barrier = pltpu.get_barrier_semaphore()
    stn_peers = [lax.rem(my_block + d, blocks) for d in range(1, blocks)]
    freq_peers = [lax.rem(my_band + d, bands) for d in range(1, bands)]
    slots = bands * blocks
    my_slot = my_band * blocks + my_block

    def slot_device(distance):
        slot = lax.rem(my_slot + distance, slots)
        return (slot // blocks, lax.rem(slot, blocks))

    def each_distance(act):
        if slots <= 32:
            for distance in range(1, slots):
                act(distance)
        else:
            pl.loop(1, slots)(act)

    @each_distance
    def greet(distance):
        pl.semaphore_signal(
            barrier, inc=1, device_id=slot_device(distance), device_id_type=MESH
        )

    def send(source, target, ssem, rsem, at, device):
        copy = pltpu.make_async_remote_copy(
            src_ref=source,
            dst_ref=target,
            send_sem=ssem.at[at],
            recv_sem=rsem.at[at],
            device_id=device,
            device_id_type=MESH,
        )
        copy.start()
        return copy

    def to_blocks(source_of, target, ssem, rsem):
        return [
            send(source_of(peer), target.at[my_block], ssem, rsem, at, (my_band, peer))
            for at, peer in enumerate(stn_peers)
        ]

    def to_bands(target, ssem, rsem, first=0):
        return [
            send(target, target, ssem, rsem, first + at, (peer, my_block))
            for at, peer in enumerate(freq_peers)
        ]

    def norm_copy(distance):
        return pltpu.make_async_remote_copy(
            src_ref=norm_all.at[my_slot],
            dst_ref=norm_all.at[my_slot],
            send_sem=norm_ssem.at[distance],
            recv_sem=norm_rsem.at[distance],
            device_id=slot_device(distance),
            device_id_type=MESH,
        )

    gains = gains_ref[...]
    half = 4 * DIRS
    near_all[my_block] = jnp.concatenate(
        [gains[0:4].reshape(half, rows), gains[4:8].reshape(half, rows)], 1
    )
    own_jones = by_station(gains)
    place_all[my_block] = jnp.zeros((8, 2 * rows), F32)
    place_all[my_block, 0:3, 0:rows] = stations_ref[...]
    base_all[my_band] = own_jones + by_station(duals_ref[...])

    mask = mask_ref[...].astype(F32)
    for pair in range(5):
        if pair < 4:
            first, second = vis_ref[2 * pair] * mask, vis_ref[2 * pair + 1] * mask
        else:
            first = second = mask
        turned = jnp.concatenate([first, second], 0).T.astype(BF16)
        for block in range(blocks):
            vis_send[block, pair] = turned[block * rows : (block + 1) * rows]
        if pair < 4:
            wide[2 * pair] = first
            wide[2 * pair + 1] = second
        else:
            mask_sum[...] = first
    pl.semaphore_wait(barrier, slots - 1)
    place_copies = to_blocks(
        lambda peer: place_all.at[my_block], place_all, place_ssem, place_rsem
    )
    near_copies = to_blocks(lambda peer: near_all.at[my_block], near_all, near_ssem, near_rsem)
    vis_copies = to_blocks(lambda peer: vis_send.at[peer], vis_recv, vis_ssem, vis_rsem)
    base_copies = to_bands(base_all.at[my_band], base_ssem, base_rsem)
    vis_recv[my_block] = vis_send[my_block]

    clusters = clusters_ref[...].reshape(1, comps)
    member = (lax.broadcasted_iota(jnp.int32, (DIRS, comps), 0) == clusters).astype(F32)
    chunks = comps // LANES
    stacked = jnp.concatenate([member[:, c * LANES : (c + 1) * LANES] for c in range(chunks)], 0)
    before = (
        lax.broadcasted_iota(jnp.int32, (LANES, LANES), 0)
        < lax.broadcasted_iota(jnp.int32, (LANES, LANES), 1)
    ).astype(BF16)
    prefix = jnp.dot(stacked.astype(BF16), before, preferred_element_type=F32)
    running = jnp.zeros((DIRS, 1), F32)
    rank_iota = lax.broadcasted_iota(jnp.int32, (LANES, LANES), 0).astype(F32)
    for c in range(chunks):
        own = stacked[c * DIRS : (c + 1) * DIRS]
        rank = jnp.sum(own * (prefix[c * DIRS : (c + 1) * DIRS] + running), 0, keepdims=True)
        oh_rank[:, c * LANES : (c + 1) * LANES] = (rank_iota == rank).astype(BF16)
        running = running + jnp.sum(own, 1, keepdims=True)
    values = jnp.concatenate(
        [
            dirs_ref[...],
            flux_ref[...].reshape(1, comps),
            pol_ref[...],
            index_ref[...].reshape(1, comps),
            jnp.zeros((2, comps), F32),
        ],
        0,
    )
    high = values.astype(BF16).astype(F32)
    middle = (values - high).astype(BF16).astype(F32)
    low = values - high - middle
    parts = jnp.concatenate([high, middle, low, jnp.zeros_like(low)], 0)
    for k in range(DIRS):
        sky_lhs[32 * k : 32 * k + 32] = (member[k : k + 1] * parts).astype(BF16)
    sky = lax.dot_general(
        sky_lhs[...], oh_rank[...], (((1,), (1,)), ((), ())), preferred_element_type=F32
    ).reshape(DIRS, 4, 8, LANES)
    sky = (sky[:, 2] + sky[:, 1]) + sky[:, 0]
    band_number = my_band.astype(F32)
    ratio = 0.5 + 3.0 * (band_number + 0.5) / bands
    l_all, m_all, i_all, q_all, u_all, slope = (sky[:, at] for at in range(6))
    factor = jnp.exp(slope * jnp.log(jnp.full((DIRS, LANES), ratio, F32)))
    n_all = jnp.sqrt(1.0 - l_all * l_all - m_all * m_all) - 1.0
    sky_rows[:, 0] = l_all
    sky_rows[:, 1] = m_all
    sky_rows[:, 2] = n_all
    sky_rows[:, 3] = (i_all + q_all) * factor
    sky_rows[:, 4] = u_all * factor
    sky_rows[:, 5] = (i_all - q_all) * factor
    sky_rows[:, 6] = n_all
    sky_rows[:, 7] = n_all
    sky_turned = sky_rows[...].reshape(DIRS * 8, LANES).T
    for k in range(DIRS):
        sky_cols[k] = sky_turned[:, 8 * k : 8 * k + 8]
        jones_cols[k] = gains[:, k, :].T
    zero_rows = jnp.zeros((LANES - span, 2 * total), BF16)
    for right in (right_even, right_odd):
        right[span:LANES] = zero_rows
        right[LANES + span :] = zero_rows
    own_place = stations_ref[...].T * ratio

    def geometry(l_value, m_value, n_value, places):
        return l_value * places[0] + m_value * places[1] + n_value * places[2]

    @pl.loop(0, DIRS, unroll=4)
    def build_left(k):
        row = sky_rows[k]
        near = jones_cols[k]
        for at in range(8):
            jones_near[k, at] = jnp.broadcast_to(near[:, at : at + 1], (rows, LANES))
        step = 2 * BF16_ROWS
        for low in range(0, rows, step):
            places = [own_place[low : low + step, a : a + 1] for a in range(3)]
            turns = geometry(row[0:1], row[1:2], row[2:3], places)
            own_r, own_i = (value.astype(F32) for value in phasor(turns))
            for at in range(3):
                weight = row[3 + at : 4 + at]
                cut = slice(at * rows + low, at * rows + low + step)
                left_all[k, cut, 0:LANES] = (own_r * weight).astype(BF16)
                left_all[k, cut, LANES:] = (own_i * weight).astype(BF16)

    for copy in place_copies:
        copy.wait()
    for block in range(blocks):
        place_rows[:, block * rows : (block + 1) * rows] = place_all[block, :, 0:rows] * ratio

    def build(k, right):
        step = 2 * BF16_ROWS
        places = [place_rows[a : a + 1, :] for a in range(3)]
        low = 0
        while low < span:
            high = min(low + step, span)
            l_col, m_col, n_col = (sky_cols[k, low:high, at : at + 1] for at in range(3))
            for tile in range(0, total, LANES):
                lanes = slice(tile, tile + LANES)
                turns = geometry(l_col, m_col, n_col, [place[:, lanes] for place in places])
                far_r, far_i = phasor(turns)
                right[low:high, lanes] = far_r
                right[low:high, total + tile : total + tile + LANES] = -far_i
                right[LANES + low : LANES + high, lanes] = far_i
                right[LANES + low : LANES + high, total + tile : total + tile + LANES] = far_r
            low = high

    def multiply(k, right):
        coh[k] = jnp.dot(left_all[k], right[...], preferred_element_type=F32)

    build(0, right_even)

    @pl.loop(0, DIRS // 2 - 1)
    def coherencies(at):
        build(2 * at + 1, right_odd)
        multiply(2 * at, right_even)
        build(2 * at + 2, right_even)
        multiply(2 * at + 1, right_odd)

    build(DIRS - 1, right_odd)
    multiply(DIRS - 2, right_even)
    multiply(DIRS - 1, right_odd)

    for copy in near_copies:
        copy.wait()
    for block in range(blocks):
        cut = slice(block * rows, (block + 1) * rows)
        near = near_all[block]
        jones_rows[0:4, :, cut] = near[:, 0:rows].reshape(4, DIRS, rows)
        jones_rows[4:8, :, cut] = near[:, rows:].reshape(4, DIRS, rows)
    for k in range(DIRS):
        for at in range(8):
            jones_far[k, at] = jnp.broadcast_to(jones_rows[at, k : k + 1, :], (8, total))
    def finish_wide():
        for copy in vis_copies:
            copy.wait()
        for i in range(2):
            for j in range(2):
                for part in range(2):
                    lanes = slice(part * rows, (part + 1) * rows)
                    other = jnp.concatenate(
                        [vis_recv[block, 2 * j + i, :, lanes].astype(F32) for block in range(blocks)],
                        1,
                    )
                    at = 2 * (2 * i + j) + part
                    wide[at] = wide[at] + other if part == 0 else wide[at] - other
        mask_sum[...] += jnp.concatenate(
            [vis_recv[block, 4, :, 0:rows].astype(F32) for block in range(blocks)], 1
        )

    lane = lax.broadcasted_iota(jnp.int32, (8, 8 * DIRS), 1)

    kept = far_terms.shape[2]
    tiles = [slice(tile, tile + LANES) for tile in range(0, total, LANES)]

    def model_rows(row_at):
        cut = pl.ds(pl.multiple_of(row_at * 8, 8), 8)
        kept_cut = cut if kept == rows else slice(0, 8)

        def add_model(k, sums):
            near = [jones_near[k, at, cut] for at in range(8)]
            done = []
            for tile, lanes in enumerate(tiles):
                far_lanes = slice(total + tile * LANES, total + (tile + 1) * LANES)
                entries = []
                for at in range(3):
                    rows_at = pl.ds(pl.multiple_of(at * rows + row_at * 8, 8), 8)
                    entries.append((coh[k, rows_at, lanes], coh[k, rows_at, far_lanes]))
                matrix = ((entries[0], entries[1]), (entries[1], entries[2]))
                own = list(sums[8 * tile : 8 * tile + 8])
                for el in range(2):
                    c_r, c_i, d_r, d_i = (jones_far[k, 4 * el + a, :, lanes] for a in range(4))
                    for m in range(2):
                        (a_r, a_i), (b_r, b_i) = matrix[m]
                        y_r = (a_r * c_r + a_i * c_i) + (b_r * d_r + b_i * d_i)
                        y_i = (a_i * c_r - a_r * c_i) + (b_i * d_r - b_r * d_i)
                        far_terms[k, 4 * m + 2 * el, kept_cut, lanes] = y_r
                        far_terms[k, 4 * m + 2 * el + 1, kept_cut, lanes] = y_i
                        for i in range(2):
                            p_r, p_i = near[4 * i + 2 * m], near[4 * i + 2 * m + 1]
                            at = 4 * i + 2 * el
                            own[at] = own[at] + (p_r * y_r - p_i * y_i)
                            own[at + 1] = own[at + 1] + (p_r * y_i + p_i * y_r)
                done += own
            return tuple(done)

        sums = lax.fori_loop(
            0,
            DIRS,
            add_model,
            tuple(jnp.zeros((8, LANES), F32) for _ in range(8 * len(tiles))),
            unroll=8,
        )
        for tile, lanes in enumerate(tiles):
            for at in range(8):
                model[at, cut, lanes] = sums[8 * tile + at]

    def gradient_rows(row_at):
        cut = pl.ds(pl.multiple_of(row_at * 8, 8), 8)
        kept_cut = cut if kept == rows else slice(0, 8)
        w = [
            [
                wide[at, cut, lanes] - mask_sum[cut, lanes] * model[at, cut, lanes]
                for at in range(8)
            ]
            for lanes in tiles
        ]

        def add_gradient(k, columns):
            totals = [None] * 8
            for tile, lanes in enumerate(tiles):
                y = [far_terms[k, at, kept_cut, lanes] for at in range(8)]
                for i in range(2):
                    for j in range(2):
                        at = 4 * i + 2 * j
                        for m in range(2):
                            w_r, w_i = w[tile][4 * i + 2 * m], w[tile][4 * i + 2 * m + 1]
                            y_r, y_i = y[4 * j + 2 * m], y[4 * j + 2 * m + 1]
                            both = (w_r * y_r + w_i * y_i, w_i * y_r - w_r * y_i)
                            for part in range(2):
                                old = totals[at + part]
                                totals[at + part] = both[part] if old is None else old + both[part]
            for at in range(8):
                summed = jnp.sum(totals[at], 1, keepdims=True)
                columns = jnp.where(lane == at * DIRS + k, summed, columns)
            return columns

        grad_cols[cut] = lax.fori_loop(
            0, DIRS, add_gradient, jnp.zeros((8, 8 * DIRS), F32), unroll=16
        )

    centre = (2.0 * band_number + 1.0) / bands - 1.0
    basis = (
        1.0,
        centre,
        0.5 * (3.0 * centre * centre - 1.0),
        0.5 * (5.0 * centre * centre * centre - 3.0 * centre),
    )
    if kept == rows:
        pl.loop(0, rows // 8)(model_rows)
    poly = cons_ref[0]
    for i in range(1, 4):
        poly = poly + basis[i] * cons_ref[i]
    pull = PENALTY / 2.0 * (base_all[my_band] - by_station(poly))
    finish_wide()

    drive_copies = []
    squares = jnp.zeros((8, 8 * DIRS), F32)
    for part in range(2):

        @pl.loop(part * rows // 16, (part + 1) * rows // 16)
        def gradient(row_at):
            if kept != rows:
                model_rows(row_at)
            gradient_rows(row_at)

        cut = slice(part * rows // 2, (part + 1) * rows // 2)
        piece = pull[cut] - grad_cols[cut]
        drive_all[my_band, cut] = piece
        squares = squares + jnp.sum((piece * piece).reshape(-1, 8, 8 * DIRS), 0)
        if part == 1:
            norm_all[my_slot] = jnp.sum(squares, 0, keepdims=True)

            @each_distance
            def send_norms(distance):
                norm_copy(distance).start()

        drive_copies += to_bands(
            drive_all.at[my_band, cut], drive_ssem, drive_rsem, part * (bands - 1)
        )

    @each_distance
    def wait_norms(distance):
        norm_copy(distance).wait()

    squares = jnp.concatenate(
        [jnp.sum(norm_all[band * blocks : (band + 1) * blocks], 0) for band in range(bands)], 0
    )
    mean = jnp.sum(squares, 1, keepdims=True) / (8 * DIRS * total)
    steps = STEP_SIZE / jnp.sqrt(mean + 1e-06)
    for copy in base_copies + drive_copies:
        copy.wait()
    sums = [
        base_all[band] - steps[band : band + 1] * drive_all[band] for band in range(bands)
    ]
    table = basis_rows(bands)
    solve = np.linalg.solve(table.T @ table, table.T)
    fitted = None
    for i in range(4):
        value = float(solve[i, 0]) * sums[0]
        for band in range(1, bands):
            value = value + float(solve[i, band]) * sums[band]
        result[2 + i] = value
        fitted = value if i == 0 else fitted + basis[i] * value
    squares = jnp.sum(norm_all[pl.ds(my_band * blocks, blocks)], 0)
    mean = jnp.sum(squares, 1, keepdims=True) / (8 * DIRS * total)
    move = STEP_SIZE / jnp.sqrt(mean + 1e-06) * drive_all[my_band]
    result[0] = own_jones - move
    result[1] = base_all[my_band] - move - fitted


def spread(result, jones_out, duals_out, cons_out):
    shape = jones_out.shape
    jones_out[...] = result[0].T.reshape(shape)
    duals_out[...] = result[1].T.reshape(shape)
    for i in range(4):
        cons_out[i] = result[2 + i].T.reshape(shape)


def local(
    visibilities,
    flag_mask,
    stations,
    directions,
    intensity,
    polarized,
    spectral,
    clusters,
    jones_gains,
    scaled_duals,
    consensus,
):
    bands = lax.axis_size("freq")
    blocks = lax.axis_size("stn")
    rows, total = flag_mask.shape
    comps = clusters.shape[0]
    kept = rows if DIRS * 8 * rows * total * 4 <= 2**24 else 8
    vmem = pl.BlockSpec(memory_space=pltpu.VMEM)
    block_sem = pltpu.SemaphoreType.DMA((blocks - 1,))
    band_sem = pltpu.SemaphoreType.DMA((bands - 1,))
    result = pl.pallas_call(
        functools.partial(kernel, bands, blocks),
        out_shape=jax.ShapeDtypeStruct((6, rows, 8 * DIRS), F32),
        in_specs=[vmem] * 11,
        out_specs=vmem,
        scratch_shapes=[
            pltpu.VMEM((blocks, 4 * DIRS, 2 * rows), F32),
            pltpu.VMEM((blocks, 8, 2 * rows), F32),
            pltpu.VMEM((blocks, 5, rows, 2 * rows), BF16),
            pltpu.VMEM((blocks, 5, rows, 2 * rows), BF16),
            pltpu.VMEM((bands, rows, 8 * DIRS), F32),
            pltpu.VMEM((bands, rows, 8 * DIRS), F32),
            pltpu.VMEM((bands * blocks, 1, 8 * DIRS), F32),
            pltpu.VMEM((LANES, comps), BF16),
            pltpu.VMEM((32 * DIRS, comps), BF16),
            pltpu.VMEM((DIRS, 8, LANES), F32),
            pltpu.VMEM((DIRS, LANES, 8), F32),
            pltpu.VMEM((DIRS, rows, 8), F32),
            pltpu.VMEM((DIRS, 8, rows, LANES), F32),
            pltpu.VMEM((8, DIRS, total), F32),
            pltpu.VMEM((DIRS, 8, 8, total), F32),
            pltpu.VMEM((8, total), F32),
            pltpu.VMEM((DIRS, 3 * rows, 2 * LANES), BF16),
            pltpu.VMEM((2 * LANES, 2 * total), BF16),
            pltpu.VMEM((2 * LANES, 2 * total), BF16),
            pltpu.VMEM((DIRS, 3 * rows, 2 * total), F32),
            pltpu.VMEM((DIRS, 8, kept, total), F32),
            pltpu.VMEM((8, rows, total), F32),
            pltpu.VMEM((8, rows, total), F32),
            pltpu.VMEM((rows, total), F32),
            pltpu.VMEM((rows, 8 * DIRS), F32),
        ]
        + [block_sem] * 6
        + [pltpu.SemaphoreType.DMA((bands * blocks,))] * 2
        + [band_sem] * 2
        + [pltpu.SemaphoreType.DMA((2 * (bands - 1),))] * 2,
        compiler_params=pltpu.CompilerParams(
            collective_id=0, has_side_effects=True, vmem_limit_bytes=58 * 1024 * 1024
        ),
    )(
        visibilities[0],
        flag_mask,
        stations,
        directions,
        intensity,
        polarized,
        spectral,
        clusters,
        jones_gains[0],
        scaled_duals[0],
        consensus,
    )
    outs = pl.pallas_call(
        spread,
        out_shape=(
            jax.ShapeDtypeStruct((8, DIRS, rows), F32),
            jax.ShapeDtypeStruct((8, DIRS, rows), F32),
            jax.ShapeDtypeStruct((4, 8, DIRS, rows), F32),
        ),
        in_specs=[vmem],
        out_specs=(vmem, vmem, vmem),
    )(result)
    return (outs[0][None], outs[1][None], outs[2])


def solution(mesh):
    placed = (
        P("freq", None, "stn", None),
        P("stn", None),
        P(None, "stn"),
        P(),
        P(),
        P(),
        P(),
        P(),
        P("freq", None, None, "stn"),
        P("freq", None, None, "stn"),
        P(None, None, None, "stn"),
    )
    return jax.shard_map(
        local,
        mesh=mesh,
        in_specs=placed,
        out_specs=(
            P("freq", None, None, "stn"),
            P("freq", None, None, "stn"),
            P(None, None, None, "stn"),
        ),
        check_vma=False,
    )
```
